256 devices in a mesh: mem: 8 (over z_hi, y), row: 32 (over x, z_lo, core).
Axes of the slice: x: 4, y: 4, z: 8 (z_hi: 2, z_lo: 4; z = z_hi * 4 + z_lo), core: 2. Of those that a mesh axis runs over, the one named last changes fastest.
Arguments:
- members: bfloat16 [128, 8, 2, 256, 512], P('mem', None, None, 'row'), may hold values from -6 to 6
- static_scale: float32 [8, 2, 256, 512], P('mem', None, 'row'), may hold values from 0.3 to 1.5
- observed: float32 [8, 2, 256, 512], P('mem', None, 'row'), may hold values from -5 to 5, as said below
- huber_class: int32 [8, 2, 256, 512], P('mem', None, 'row'), may hold values from 0 to 3
- scale_index: int32 [2, 256, 512], P(None, 'row'), may hold values from 0 to 3
Outputs:
- control: float32 [128, 2, 256, 512], P('mem', None, 'row')
- static_control: float32 [8, 2, 256, 512], P('mem', None, 'row')
- increment: float32 [8, 2, 256, 512], P('mem', None, 'row')
The draws below stay inside these ranges and needn't reach their ends.
Inputs may be any that keep to these rules, and one draw needn't show every extreme that they name: observed departures of order one.
All inputs are finite; a program needn't handle non-finite values.
Results may differ from the reference program's by a relative error of at most 0.0035.
Values may be sent and summed in bfloat16 or wider, within the bound.
A program may use at most 64 MiB of HBM per device.

```python
import math
import jax
import jax.numpy as jnp
from jax import lax

VARS = 8
LEVELS = 2
NX = 512
SWEEPS = 4
ITERS = 2
ENSEMBLE = 128
NY = 256


def draw_observed(key, part):
    first = jax.random.fold_in(jax.random.fold_in(key, 17), 0)
    row_frac = jnp.arange(NY, dtype=jnp.float32) / max(NY - 1, 1)
    var_frac = jnp.arange(VARS, dtype=jnp.float32) / max(VARS - 1, 1)
    scale = (0.5 + row_frac)[None, None, :, None] * (0.7 + 0.6 * var_frac)[:, None, None, None]
    value = jax.random.normal(first, (VARS, LEVELS, NY, NX), jnp.float32) * scale
    return jnp.clip(value, -5.0, 5.0)


def place_ends(array, rng, least, high):
    dims = array.shape
    index_at = [jax.random.randint(jax.random.fold_in(rng, axis), (), 0, dims[axis]) for axis in range(len(dims))]
    array = array.at[tuple(index_at)].set(least)
    longest = dims.index(max(dims))
    index_at[longest] = (index_at[longest] + 1) % dims[longest]
    return array.at[tuple(index_at)].set(high)


def levels(stream_key, extent, cuts, least, top_value):
    def one(position, parts):
        heights = jax.random.uniform(jax.random.fold_in(jax.random.fold_in(stream_key, 6), position), (parts,), jnp.float32, least / len(cuts), top_value / len(cuts))
        return jnp.repeat(jnp.exp(heights), extent[position] // parts).reshape((-1,) + (1,) * (len(extent) - position - 1))

    factor_of = one(*cuts[0])
    for cut in cuts[1:]:
        factor_of = factor_of * one(*cut)
    return factor_of


def scatter_about(own_key, dims, scale, most, cuts=(), kind=jnp.bfloat16):
    level = levels(own_key, dims, cuts, -0.22, 0.18) if cuts else 1.0
    array = jax.random.normal(own_key, dims, jnp.float32) * scale * level
    return jnp.minimum(jnp.maximum(array, -most), most).astype(kind)


def setup_inputs(seed: int = 0) -> dict:
    streams_of = jax.random.split(jax.random.key(seed), 6)
    members = scatter_about(streams_of[0], (ENSEMBLE, VARS, LEVELS, NY, NX), 1.0, 6.0, ((0, 8), (3, 32)))
    static_scale = jnp.clip(jnp.exp(math.log(1.5) - 1.60943787 * jax.random.uniform(streams_of[1], (VARS, LEVELS, NY, NX), jnp.float32) ** levels(streams_of[1], (VARS, LEVELS, NY, NX), ((0, 8), (2, 32)), -0.2, 0.2)), 0.3, 1.5)
    observed = draw_observed(jax.random.fold_in(streams_of[5], 71), 0)
    huber_class = place_ends(jax.random.randint(streams_of[3], (VARS, LEVELS, NY, NX), 0, 4), jax.random.fold_in(streams_of[3], 1), 0, 3).astype(jnp.int32)
    scale_index = place_ends(jax.random.randint(streams_of[4], (LEVELS, NY, NX), 0, 4), jax.random.fold_in(streams_of[4], 1), 0, 3).astype(jnp.int32)
    return dict(members=members, static_scale=static_scale, observed=observed, huber_class=huber_class, scale_index=scale_index)


kappa_table = (0.06, 0.11, 0.17, 0.23)
huber_levels = (1.0, 0.5, 1.0, 2.0)

def kappa_field(scale_index):
    result = jnp.zeros(scale_index.shape, jnp.float32)
    for level_id in range(4):
        result = result + jnp.where(scale_index == level_id, kappa_table[level_id], 0.0).astype(jnp.float32)
    return result

def threshold_field(huber_class):
    result = jnp.zeros(huber_class.shape, jnp.float32)
    for level_id in range(4):
        result = result + jnp.where(huber_class == level_id, huber_levels[level_id], 0.0).astype(jnp.float32)
    return result

def laplace(padded):
    full = jnp.pad(padded, [(0, 0)] * (padded.ndim - 1) + [(1, 1)])
    centre = full[..., 1:-1, 1:-1]
    vertical = full[..., 2:, 1:-1] + full[..., :-2, 1:-1]
    sideways = full[..., 1:-1, 2:] + full[..., 1:-1, :-2]
    return vertical + sideways - 4.0 * centre

def pad_rows(field):
    return jnp.pad(field, [(0, 0)] * (field.ndim - 2) + [(1, 1), (0, 0)])

def forward(field, kappa):
    for sweep in range(SWEEPS):
        field = field + kappa * laplace(pad_rows(field))
    return field

def adjoint(field, kappa):
    for sweep in range(SWEEPS):
        field = field + laplace(pad_rows(kappa * field))
    return field

def reference(members, static_scale, observed, huber_class, scale_index):
    kappa = kappa_field(scale_index)
    threshold = threshold_field(huber_class)
    observed_mask = (huber_class > 0).astype(jnp.float32)
    ens_coef = math.sqrt(0.7 / (ENSEMBLE - 1))
    stat_coef = math.sqrt(0.3)
    control = jnp.zeros((ENSEMBLE, LEVELS, NY, NX), jnp.float32)
    static_control = jnp.zeros((VARS, LEVELS, NY, NX), jnp.float32)
    increment = jnp.zeros((VARS, LEVELS, NY, NX), jnp.float32)
    for turn in range(ITERS):
        misfit = increment - observed
        clipped = observed_mask * jnp.clip(misfit, -threshold, threshold)
        weight = observed_mask * threshold / jnp.maximum(jnp.abs(misfit), threshold)
        sent = clipped.astype(jnp.bfloat16)
        sent_wide = sent.astype(jnp.float32)
        back = lax.map(lambda member: ens_coef * lax.optimization_barrier(jnp.sum(member.astype(jnp.float32) * sent_wide, axis=0)), members)
        grad_ens = control + lax.map(lambda field: adjoint(field, kappa), back)
        grad_stat = static_control + adjoint(stat_coef * static_scale * sent_wide, kappa)
        norm = jnp.sum(grad_ens * grad_ens) + jnp.sum(grad_stat * grad_stat)
        spread = lax.map(lambda field: forward(field, kappa), grad_ens).astype(jnp.bfloat16)

        def accumulate(total, pair):
            member, piece = pair
            return (total + member.astype(jnp.float32) * piece.astype(jnp.float32)[None], None)
        summed, unused = lax.scan(accumulate, jnp.zeros((VARS, LEVELS, NY, NX), jnp.float32), (members, spread))
        image = ens_coef * summed + stat_coef * static_scale * forward(grad_stat, kappa)
        curvature = jnp.sum(weight * image * image)
        step = norm / (norm + curvature)
        control = control - step * grad_ens
        static_control = static_control - step * grad_stat
        increment = increment - step * image
    return (control, static_control, increment)
```

```python
import functools
import math

import jax
import jax.numpy as jnp
from jax import lax
from jax.experimental import pallas as pl
from jax.experimental.pallas import tpu as pltpu
from jax.sharding import PartitionSpec as P

SWEEPS = 4
ITERS = 2
KAPPAS = (0.06, 0.11, 0.17, 0.23)
LANES = 128
STAT = math.sqrt(0.3)
MESH = pl.DeviceIdType.MESH


def sideways(w):
    lane = lax.broadcasted_iota(jnp.int32, w.shape[1:], 1)[None]
    edge = jnp.zeros_like(w[:1])
    right = pltpu.roll(w, 1, 2)
    left = pltpu.roll(w, LANES - 1, 2)
    from_left = jnp.where(lane == 0, jnp.concatenate([edge, right[:-1]], 0), right)
    from_right = jnp.where(lane == LANES - 1, jnp.concatenate([left[1:], edge], 0), left)
    return from_left + from_right


def kernel(
    n_mem, n_row, ens_coef,
    members_h, scale_h, observed_h, huber_h, index_h,
    control_o, static_o, increment_o,
    members, scale, observed, huber, index,
    sent_all, send_static, static_halo, send_index, index_halo,
    kwide, knat, turned, field, send_back, back_halo,
    grad, control, spread, partial, arrived,
    stat_grad, stat_control, stat_part, image, increment, norm_acc, first, second,
    load_sem, done_sem, sent_send, sent_recv, halo_send, halo_recv, part_send, part_recv,
    small_send, small_recv,
):
    me_m = lax.axis_index("mem")
    me_r = lax.axis_index("row")
    rows = 8
    tiles = 4
    has_low = me_r > 0
    has_high = me_r < n_row - 1

    def to(m, r):
        return {"mem": m, "row": r}

    loads = [
        pltpu.make_async_copy(observed_h, observed, load_sem.at[0]),
        pltpu.make_async_copy(huber_h, huber, load_sem.at[1]),
        pltpu.make_async_copy(index_h, index, load_sem.at[2]),
        pltpu.make_async_copy(scale_h, scale, load_sem.at[3]),
    ] + [
        pltpu.make_async_copy(
            members_h.at[:, :, :, pl.ds(j * LANES, LANES)], members.at[j], load_sem.at[4 + j]
        )
        for j in range(tiles)
    ]
    for load in loads:
        load.start()

    core = lax.rem(me_r, 2)
    pair = me_r // 2
    n_first = n_mem * 2
    n_second = n_row // 2
    my_first = me_m * 2 + core

    def first_peer(d):
        other = lax.rem(my_first + d, n_first)
        return other // 2, pair * 2 + lax.rem(other, 2)

    def second_peer(d):
        return me_m, lax.rem(pair + d, n_second) * 2 + core

    barrier = pltpu.get_barrier_semaphore()
    for d in range(1, n_first):
        pl.semaphore_signal(barrier, inc=1, device_id=to(*first_peer(d)), device_id_type=MESH)
    for d in range(1, n_second):
        pl.semaphore_signal(barrier, inc=1, device_id=to(*second_peer(d)), device_id_type=MESH)
    far = jnp.where(core == 0, me_r - 1, me_r + 1)
    has_far = jnp.logical_and(far >= 0, far < n_row)

    @pl.when(has_far)
    def _():
        pl.semaphore_signal(barrier, inc=1, device_id=to(me_m, far), device_id_type=MESH)

    def lane_tile(ref, l, j):
        return ref[l, :, j * LANES:(j + 1) * LANES]

    def cutoff(l, j):
        h = lane_tile(huber, l, j)
        return jnp.where(h == 1, 0.5, jnp.where(h == 2, 1.0, jnp.where(h == 3, 2.0, 0.0))).astype(
            jnp.float32
        )

    for load in loads[:4]:
        load.wait()
    increment[...] = jnp.zeros_like(increment)
    control[...] = jnp.zeros_like(control)
    stat_control[...] = jnp.zeros_like(stat_control)
    for j in range(tiles):
        send_index[j] = jnp.concatenate(
            [lane_tile(index, 0, j), lane_tile(index, 1, j)], 0
        ).astype(jnp.float32).astype(jnp.bfloat16)

    @pl.when(jnp.logical_not(has_low))
    def _():
        index_halo[0] = jnp.full(index_halo.shape[1:], -1.0, jnp.bfloat16)
        static_halo[:, 0] = jnp.zeros_like(static_halo[:, 0])
        for it in range(ITERS):
            for l in range(2):
                back_halo[it, 0, l] = jnp.zeros_like(back_halo[it, 0, l])

    @pl.when(jnp.logical_not(has_high))
    def _():
        index_halo[1] = jnp.full(index_halo.shape[1:], -1.0, jnp.bfloat16)
        static_halo[:, 1] = jnp.zeros_like(static_halo[:, 1])
        for it in range(ITERS):
            for l in range(2):
                back_halo[it, 1, l] = jnp.zeros_like(back_halo[it, 1, l])

    def make_sent(it):
        for j in range(tiles):
            parts = []
            for l in range(2):
                cut = cutoff(l, j)
                misfit = increment[l, j] - lane_tile(observed, l, j)
                parts.append(jnp.minimum(jnp.maximum(misfit, -cut), cut))
            value = jnp.concatenate(parts, 0).astype(jnp.bfloat16)
            sent_all[it, me_m, j] = value
            wide = value.astype(jnp.float32)
            for l in range(2):
                stat = STAT * lane_tile(scale, l, j) * wide[l * rows:(l + 1) * rows]
                field_stat = stat
                image[l, j] = field_stat
            send_static[it, j] = jnp.concatenate([image[0, j], image[1, j]], 0).astype(jnp.bfloat16)

    def rowcopy(src, dst_at, slot, side):
        target = me_r + 1 if side == 0 else me_r - 1
        return pltpu.make_async_remote_copy(
            src_ref=src, dst_ref=dst_at(side), send_sem=halo_send.at[slot, side],
            recv_sem=halo_recv.at[slot, side], device_id=to(me_m, target), device_id_type=MESH,
        )

    def row_start(src, dst_at, slot):
        @pl.when(has_high)
        def _():
            rowcopy(src, dst_at, slot, 0).start()

        @pl.when(has_low)
        def _():
            rowcopy(src, dst_at, slot, 1).start()

    def row_wait(src, dst_at, slot):
        @pl.when(has_low)
        def _():
            rowcopy(src, dst_at, slot, 0).wait_recv()

        @pl.when(has_high)
        def _():
            rowcopy(src, dst_at, slot, 1).wait_recv()

    def row_wait_send(src, dst_at, slot):
        @pl.when(has_high)
        def _():
            rowcopy(src, dst_at, slot, 0).wait_send()

        @pl.when(has_low)
        def _():
            rowcopy(src, dst_at, slot, 1).wait_send()

    n_slot = 3
    index_args = (send_index, lambda side: index_halo.at[side], ITERS * n_slot)

    def static_args(it):
        return send_static.at[it], lambda side: static_halo.at[it, side], it * n_slot

    def back_args(it, l):
        return send_back.at[it, l], lambda side: back_halo.at[it, side, l], it * n_slot + 1 + l

    def gather_copy(it, d):
        return pltpu.make_async_remote_copy(
            src_ref=sent_all.at[it, me_m], dst_ref=sent_all.at[it, me_m],
            send_sem=sent_send.at[it], recv_sem=sent_recv.at[it],
            device_id=to(lax.rem(me_m + d, n_mem), me_r), device_id_type=MESH,
        )

    def part_copy(it, l, d):
        v = lax.rem(me_m + d, n_mem)
        return pltpu.make_async_remote_copy(
            src_ref=partial.at[it, l, v], dst_ref=arrived.at[it, l, me_m],
            send_sem=part_send.at[it, l], recv_sem=part_recv.at[it, l],
            device_id=to(v, me_r), device_id_type=MESH,
        )

    def first_copy(it, d):
        m, r = first_peer(d)
        return pltpu.make_async_remote_copy(
            src_ref=first.at[it, my_first], dst_ref=first.at[it, my_first],
            send_sem=small_send.at[it, 0], recv_sem=small_recv.at[it, 0],
            device_id=to(m, r), device_id_type=MESH,
        )

    def second_copy(it, d):
        m, r = second_peer(d)
        return pltpu.make_async_remote_copy(
            src_ref=second.at[it, pair], dst_ref=second.at[it, pair],
            send_sem=small_send.at[it, 1], recv_sem=small_recv.at[it, 1],
            device_id=to(m, r), device_id_type=MESH,
        )

    def bytes_wait(ref, count, sem):
        part = ref.at[pl.ds(0, count)]
        pltpu.make_async_copy(part, part, sem).wait()

    def diffuse(it, l, g):
        low_in = jnp.where(has_low, 1.0, 0.0).astype(jnp.float32)
        high_in = jnp.where(has_high, 1.0, 0.0).astype(jnp.float32)
        for sweep in range(SWEEPS):
            lo, hi = sweep, 3 * rows - sweep

            def get(row):
                u = field[l, row, g]
                return u, u * kwide[l, row]

            _, w_prev = get(lo)
            u_cur, w_cur = get(lo + 1)
            norm = jnp.zeros((8, LANES), jnp.float32)
            for row in range(lo + 1, hi - 1):
                u_next, w_next = get(row + 1)
                out = (w_prev + w_next) + sideways(w_cur) + (u_cur - 4.0 * w_cur)
                if sweep < SWEEPS - 1:
                    field[l, row, g] = out
                else:
                    out = out + control[l, row - SWEEPS, g]
                    if row < rows:
                        out = out * low_in
                    elif row >= 2 * rows:
                        out = out * high_in
                    else:
                        norm = norm + jnp.sum(out * out, axis=0)
                    grad[l, row - SWEEPS, g] = out
                w_prev, u_cur, w_cur = w_cur, u_next, w_next
        norm_acc[...] += norm
        for sweep in range(SWEEPS):
            lo, hi = SWEEPS + sweep, 3 * rows - SWEEPS - sweep

            def load(row):
                return grad[l, row - SWEEPS, g] if sweep == 0 else field[l, row, g]

            u_prev, u_cur = load(lo), load(lo + 1)
            for row in range(lo + 1, hi - 1):
                u_next = load(row + 1)
                out = u_cur + kwide[l, row] * ((u_prev + u_next) + sideways(u_cur) - 4.0 * u_cur)
                if sweep < SWEEPS - 1:
                    field[l, row, g] = out
                else:
                    out = out.astype(jnp.bfloat16).astype(jnp.float32)
                    for j in range(tiles):
                        spread[l, j, pl.ds((row - rows) * 16 + g * 8, 8), :] = out[j]
                u_prev, u_cur = u_cur, u_next

    def diffuse_static(it, l):
        halo = static_halo[it].astype(jnp.float32)
        here = slice(l * rows, (l + 1) * rows)
        u = jnp.concatenate([halo[0, :, here], image[l], halo[1, :, here]], 1)
        k = knat[l]
        grow = me_r * rows - rows + lax.broadcasted_iota(jnp.int32, (3 * rows, LANES), 0)
        inside = jnp.logical_and(grow >= 0, grow < n_row * rows)[None]
        n = 3 * rows
        for sweep in range(SWEEPS):
            w = k * u
            u = (pltpu.roll(w, 1, 1) + pltpu.roll(w, n - 1, 1)) + sideways(w) + (u - 4.0 * w)
        u = jnp.where(inside, u + stat_control[l], 0.0)
        stat_grad[l] = u
        own = u[:, rows:2 * rows]
        norm_acc[...] += jnp.sum(own * own, axis=0)
        for sweep in range(SWEEPS):
            u = u + k * (
                (pltpu.roll(u, 1, 1) + pltpu.roll(u, n - 1, 1)) + sideways(u) - 4.0 * u
            )
        for j in range(tiles):
            stat_part[l, j] = STAT * lane_tile(scale, l, j) * u[j, rows:2 * rows]

    make_sent(0)

    @pl.when(has_far)
    def _():
        pl.semaphore_wait(barrier, n_first + n_second - 1)

    @pl.when(jnp.logical_not(has_far))
    def _():
        pl.semaphore_wait(barrier, n_first + n_second - 2)

    for it in range(ITERS):
        if it > 0:
            make_sent(it)
        for d in range(1, n_mem):
            gather_copy(it, d).start()
        if it == 0:
            row_start(*index_args)
        row_start(*static_args(it))
        norm_acc[...] = jnp.zeros_like(norm_acc)
        if it == 0:
            row_wait(*index_args)
            for j in range(tiles):
                for l in range(2):
                    here = slice(l * rows, (l + 1) * rows)
                    both = index_halo[:, j].astype(jnp.float32)
                    ids = jnp.concatenate(
                        [both[0, here], lane_tile(index, l, j).astype(jnp.float32), both[1, here]],
                        0,
                    )
                    k = jnp.zeros_like(ids)
                    for i, value in enumerate(KAPPAS):
                        k = jnp.where(ids == i, value, k)
                    knat[l, j] = k
                    for row in range(3 * rows):
                        kwide[l, row, j] = jnp.broadcast_to(k[row:row + 1], (8, LANES))
            for load in loads[4:]:
                load.wait()
        bytes_wait(sent_all.at[it], n_mem - 1, sent_recv.at[it])

        @pl.loop(0, tiles)
        def _(j):
            wide = [sent_all[it, v, j].astype(jnp.float32) for v in range(n_mem)]
            for k in range(16):
                total = members[j, k, 0].astype(jnp.float32) * wide[0]
                for v in range(1, n_mem):
                    total = total + members[j, k, v].astype(jnp.float32) * wide[v]
                total = ens_coef * total
                for l in range(2):
                    turned[l, j, k * 8:(k + 1) * 8, :] = total[l * rows:(l + 1) * rows]

        for l in range(2):
            @pl.loop(0, tiles)
            def _(j):
                for r in range(rows):
                    half = [turned[l, j, pl.ds(g * 64 + r, 8, stride=8), :] for g in range(2)]
                    for g in range(2):
                        field[l, rows + r, g, j] = half[g]
                    send_back[it, l, r, j] = jnp.concatenate(half, 0).astype(jnp.bfloat16)

            row_start(*back_args(it, l))

        row_wait(*static_args(it))
        for l in range(2):
            diffuse_static(it, l)

        for l in range(2):
            row_wait(*back_args(it, l))

            @pl.loop(0, rows)
            def _(r):
                for j in range(tiles):
                    for side in range(2):
                        value = back_halo[it, side, l, r, j].astype(jnp.float32)
                        for g in range(2):
                            field[l, side * 2 * rows + r, g, j] = value[g * 8:(g + 1) * 8]

            @pl.loop(0, 2)
            def _(g):
                diffuse(it, l, g)

            @pl.loop(0, tiles // 2)
            def _(jj):
                totals = []
                for half in range(2):
                    j = jj * 2 + half
                    total = [None] * n_mem
                    for k in range(16):
                        s = spread[l, j, pl.ds(k, 8, stride=16), :]
                        for v in range(n_mem):
                            m = members[j, k, v, l * rows:(l + 1) * rows, :].astype(jnp.float32)
                            total[v] = m * s if k == 0 else total[v] + m * s
                    totals.append(total)
                for v in range(n_mem):
                    partial[it, l, v, jj] = jnp.concatenate(
                        [totals[0][v], totals[1][v]], 0
                    ).astype(jnp.bfloat16)

            for d in range(1, n_mem):
                part_copy(it, l, d).start()
            arrived[it, l, me_m] = partial[it, l, me_m]

        curv = jnp.zeros((8, LANES), jnp.float32)
        for l in range(2):
            bytes_wait(arrived.at[it, l], n_mem - 1, part_recv.at[it, l])
            total = arrived[it, l, 0].astype(jnp.float32)
            for v in range(1, n_mem):
                total = total + arrived[it, l, v].astype(jnp.float32)
            for j in range(tiles):
                part = total[j // 2, (j % 2) * 8:(j % 2) * 8 + 8]
                img = ens_coef * part + stat_part[l, j]
                image[l, j] = img
                cut = cutoff(l, j)
                misfit = increment[l, j] - lane_tile(observed, l, j)
                weight = cut / jnp.maximum(jnp.abs(misfit), jnp.where(cut == 0.0, 1.0, cut))
                curv = curv + weight * img * img

        first[it, my_first] = jnp.concatenate(
            [
                jnp.sum(norm_acc[...], axis=0, keepdims=True),
                jnp.sum(curv, axis=0, keepdims=True),
            ],
            1,
        )
        for d in range(1, n_first):
            first_copy(it, d).start()
        bytes_wait(first.at[it], n_first - 1, small_recv.at[it, 0])
        second[it, pair] = jnp.sum(first[it], axis=0)
        for d in range(1, n_second):
            second_copy(it, d).start()
        bytes_wait(second.at[it], n_second - 1, small_recv.at[it, 1])
        sums = jnp.sum(second[it], axis=0)
        norm = jnp.sum(sums[:, :LANES], axis=1, keepdims=True)
        curvature = jnp.sum(sums[:, LANES:], axis=1, keepdims=True)
        step = jnp.broadcast_to(norm / (norm + curvature), (8, LANES))

        increment[...] = increment[...] - step * image[...]
        for l in range(2):
            for j in range(tiles):
                for third in range(3):
                    here = slice(third * 8, third * 8 + 8)
                    stat_control[l, j, here] = stat_control[l, j, here] - step * stat_grad[l, j, here]
        if it < ITERS - 1:
            @pl.loop(0, 2 * rows)
            def _(row):
                for l in range(2):
                    control[l, row] = control[l, row] - step * grad[l, row]
        else:
            @pl.loop(0, tiles)
            def _(j):
                for l in range(2):
                    for r in range(rows):
                        for g in range(2):
                            spread[l, j, r * 16 + g * 8:r * 16 + g * 8 + 8, :] = (
                                control[l, SWEEPS + r, g, j] - step * grad[l, SWEEPS + r, g, j]
                            )
            for j in range(tiles):
                for l in range(2):
                    for k in range(16):
                        control_o[k, l, :, j * LANES:(j + 1) * LANES] = spread[
                            l, j, pl.ds(k, 8, stride=16), :
                        ]

    for l in range(2):
        for j in range(tiles):
            static_o[l, :, j * LANES:(j + 1) * LANES] = stat_control[l, j, rows:2 * rows]
            increment_o[l, :, j * LANES:(j + 1) * LANES] = increment[l, j]

    row_wait_send(*index_args)
    for it in range(ITERS):
        row_wait_send(*static_args(it))
        for l in range(2):
            row_wait_send(*back_args(it, l))
            bytes_wait(arrived.at[it, l], n_mem - 1, part_send.at[it, l])
        bytes_wait(sent_all.at[it], n_mem - 1, sent_send.at[it])
        bytes_wait(first.at[it], n_first - 1, small_send.at[it, 0])
        bytes_wait(second.at[it], n_second - 1, small_send.at[it, 1])


def local(n_mem, n_row, members, static_scale, observed, huber_class, scale_index):
    k, v, _, rows, cells = members.shape
    ens_coef = math.sqrt(0.7 / (k * n_mem - 1))
    f32, bf16 = jnp.float32, jnp.bfloat16
    tiles = cells // LANES
    V = pltpu.VMEM
    scratch = [
        V((tiles, k, v, 16, LANES), bf16),
        V((2, rows, cells), f32),
        V((2, rows, cells), f32),
        V((2, rows, cells), jnp.int32),
        V((2, rows, cells), jnp.int32),
        V((ITERS, n_mem, tiles, 16, LANES), bf16),
        V((ITERS, tiles, 16, LANES), bf16),
        V((ITERS, 2, tiles, 16, LANES), bf16),
        V((tiles, 16, LANES), bf16),
        V((2, tiles, 16, LANES), bf16),
        V((2, 3 * rows, tiles, 8, LANES), f32),
        V((2, tiles, 3 * rows, LANES), f32),
        V((2, tiles, k * rows, LANES), f32),
        V((2, 3 * rows, 2, tiles, 8, LANES), f32),
        V((ITERS, 2, rows, tiles, 16, LANES), bf16),
        V((ITERS, 2, 2, rows, tiles, 16, LANES), bf16),
        V((2, 2 * rows, 2, tiles, 8, LANES), f32),
        V((2, 2 * rows, 2, tiles, 8, LANES), f32),
        V((2, tiles, k * rows, LANES), f32),
        V((ITERS, 2, n_mem, tiles // 2, 16, LANES), bf16),
        V((ITERS, 2, n_mem, tiles // 2, 16, LANES), bf16),
        V((2, tiles, 3 * rows, LANES), f32),
        V((2, tiles, 3 * rows, LANES), f32),
        V((2, tiles, rows, LANES), f32),
        V((2, tiles, rows, LANES), f32),
        V((2, tiles, rows, LANES), f32),
        V((8, LANES), f32),
        V((ITERS, n_mem * 2, 1, 2 * LANES), f32),
        V((ITERS, n_row // 2, 1, 2 * LANES), f32),
        pltpu.SemaphoreType.DMA((4 + tiles,)),
        pltpu.SemaphoreType.DMA((1,)),
        pltpu.SemaphoreType.DMA((ITERS,)),
        pltpu.SemaphoreType.DMA((ITERS,)),
        pltpu.SemaphoreType.DMA((ITERS * 3 + 1, 2)),
        pltpu.SemaphoreType.DMA((ITERS * 3 + 1, 2)),
        pltpu.SemaphoreType.DMA((ITERS, 2)),
        pltpu.SemaphoreType.DMA((ITERS, 2)),
        pltpu.SemaphoreType.DMA((ITERS, 2)),
        pltpu.SemaphoreType.DMA((ITERS, 2)),
    ]
    hbm = pl.BlockSpec(memory_space=pl.ANY)
    vmem = pl.BlockSpec(memory_space=pltpu.VMEM)
    control, static_control, increment = pl.pallas_call(
        functools.partial(kernel, n_mem, n_row, ens_coef),
        out_shape=[
            jax.ShapeDtypeStruct((k, 2, rows, cells), f32),
            jax.ShapeDtypeStruct((2, rows, cells), f32),
            jax.ShapeDtypeStruct((2, rows, cells), f32),
        ],
        in_specs=[hbm] * 5,
        out_specs=[vmem] * 3,
        scratch_shapes=scratch,
        compiler_params=pltpu.CompilerParams(
            collective_id=0, has_side_effects=True, vmem_limit_bytes=40 * 1024 * 1024
        ),
    )(
        members.reshape(k, v, 2 * rows, cells),
        static_scale[0],
        observed[0],
        huber_class[0],
        scale_index,
    )
    return control, static_control[None], increment[None]


def solution(mesh):
    sizes = dict(mesh.shape)
    placed = (
        P("mem", None, None, "row", None),
        P("mem", None, "row", None),
        P("mem", None, "row", None),
        P("mem", None, "row", None),
        P(None, "row", None),
    )
    return jax.shard_map(
        functools.partial(local, sizes["mem"], sizes["row"]),
        mesh=mesh,
        in_specs=placed,
        out_specs=(P("mem", None, "row", None),) * 3,
        check_vma=False,
    )
```

```python
import functools
import math

import jax
import jax.numpy as jnp
from jax import lax
from jax.experimental import pallas as pl
from jax.experimental.pallas import tpu as pltpu
from jax.sharding import PartitionSpec as P

SWEEPS = 4
ITERS = 2
KAPPAS = (0.06, 0.11, 0.17, 0.23)
LANES = 128
STAT = math.sqrt(0.3)
MESH = pl.DeviceIdType.MESH


def sideways(w):
    lane = lax.broadcasted_iota(jnp.int32, w.shape[1:], 1)[None]
    edge = jnp.zeros_like(w[:1])
    right = pltpu.roll(w, 1, 2)
    left = pltpu.roll(w, LANES - 1, 2)
    from_left = jnp.where(lane == 0, jnp.concatenate([edge, right[:-1]], 0), right)
    from_right = jnp.where(lane == LANES - 1, jnp.concatenate([left[1:], edge], 0), left)
    return from_left + from_right


def kernel(
    n_mem, n_row, ens_coef,
    members_h, scale_h, observed_h, huber_h, index_h,
    before_o, grad_o, stat_before_o, stat_grad_o, inc_before_o, image_o, step_o,
    members, scale, observed, huber, index,
    sent_all, send_static, static_halo, send_index, index_halo,
    obs_all, cut_all, image_all,
    kwide, knat, turned, field, send_back, back_halo,
    grad, spread, partial, arrived,
    stat_grad, stat_back, stat_part, image, increment, norm_acc, step_ref, first, second,
    load_sem, sent_send, sent_recv, halo_send, halo_recv, part_send, part_recv,
    small_send, small_recv, obs_send, obs_recv, image_send, image_recv,
):
    me_m = lax.axis_index("mem")
    me_r = lax.axis_index("row")
    rows = 8
    tiles = 4
    has_low = me_r > 0
    has_high = me_r < n_row - 1

    def to(m, r):
        return {"mem": m, "row": r}

    loads = [
        pltpu.make_async_copy(observed_h, observed, load_sem.at[0]),
        pltpu.make_async_copy(huber_h, huber, load_sem.at[1]),
        pltpu.make_async_copy(index_h, index, load_sem.at[2]),
        pltpu.make_async_copy(scale_h, scale, load_sem.at[3]),
    ] + [
        pltpu.make_async_copy(
            members_h.at[:, :, :, pl.ds(j * LANES, LANES)], members.at[j], load_sem.at[4 + j]
        )
        for j in range(tiles)
    ]
    for load in loads:
        load.start()

    z_hi, y = me_m // 4, lax.rem(me_m, 4)
    x, z_lo, core = me_r // 8, lax.rem(me_r // 2, 4), lax.rem(me_r, 2)
    z = z_hi * 4 + z_lo

    def device_at(dx, dy, dz, dc):
        zz = lax.rem(z + dz, 8)
        m = (zz // 4) * 4 + lax.rem(y + dy, 4)
        r = lax.rem(x + dx, 4) * 8 + lax.rem(zz, 4) * 2 + lax.rem(core + dc, 2)
        return m, r

    def hops(d):
        return -(min(d[0], 4 - d[0]) + min(d[1], 4 - d[1]) + min(d[2], 8 - d[2]))

    planes = [(dx, dy, 0, dc) for dx in range(4) for dy in range(4) for dc in range(2)]
    planes = sorted(planes[1:], key=hops)
    along_z = sorted([(0, 0, dz, 0) for dz in range(1, 8)], key=hops)
    same_rows = sorted([(0, dy, dz, 0) for dz in (0, 4) for dy in range(4)][1:], key=hops)
    my_plane = (x * 4 + y) * 2 + core
    n_first, n_second = 32, 8

    greeted = sorted(set(planes + along_z + same_rows), key=hops)
    barrier = pltpu.get_barrier_semaphore()
    for d in greeted:
        pl.semaphore_signal(barrier, inc=1, device_id=to(*device_at(*d)), device_id_type=MESH)
    far = jnp.where(core == 0, me_r - 1, me_r + 1)
    has_far = jnp.logical_and(far >= 0, far < n_row)

    @pl.when(has_far)
    def _():
        pl.semaphore_signal(barrier, inc=1, device_id=to(me_m, far), device_id_type=MESH)

    def lane_tile(ref, l, j):
        return ref[l, :, j * LANES:(j + 1) * LANES]

    def cutoff(l, j):
        h = lane_tile(huber, l, j)
        return jnp.where(h == 1, 0.5, jnp.where(h == 2, 1.0, jnp.where(h == 3, 2.0, 0.0))).astype(
            jnp.float32
        )

    for load in loads[:4]:
        load.wait()
    for j in range(tiles):
        send_index[j] = jnp.concatenate(
            [lane_tile(index, 0, j), lane_tile(index, 1, j)], 0
        ).astype(jnp.float32).astype(jnp.bfloat16)

    @pl.when(jnp.logical_not(has_low))
    def _():
        index_halo[0] = jnp.full(index_halo.shape[1:], -1.0, jnp.bfloat16)
        static_halo[:, 0] = jnp.zeros_like(static_halo[:, 0])
        for it in range(ITERS):
            for l in range(2):
                back_halo[it, 0, l] = jnp.zeros_like(back_halo[it, 0, l])

    @pl.when(jnp.logical_not(has_high))
    def _():
        index_halo[1] = jnp.full(index_halo.shape[1:], -1.0, jnp.bfloat16)
        static_halo[:, 1] = jnp.zeros_like(static_halo[:, 1])
        for it in range(ITERS):
            for l in range(2):
                back_halo[it, 1, l] = jnp.zeros_like(back_halo[it, 1, l])

    def static_source(it):
        for j in range(tiles):
            wide = sent_all[it, me_m, j].astype(jnp.float32)
            for l in range(2):
                stat_back[l, j] = STAT * lane_tile(scale, l, j) * wide[l * rows:(l + 1) * rows]
            send_static[it, j] = jnp.concatenate(
                [stat_back[0, j], stat_back[1, j]], 0
            ).astype(jnp.bfloat16)

    def first_sent():
        for j in range(tiles):
            cut = jnp.concatenate([cutoff(0, j), cutoff(1, j)], 0)
            seen = jnp.concatenate([lane_tile(observed, 0, j), lane_tile(observed, 1, j)], 0)
            obs_all[me_m, j] = seen
            cut_all[me_m, j] = cut.astype(jnp.bfloat16)
            sent_all[0, me_m, j] = jnp.minimum(jnp.maximum(0.0 - seen, -cut), cut).astype(
                jnp.bfloat16
            )

    def next_sent(it, step):
        both = jnp.concatenate([step, step], 0)

        @pl.loop(0, n_mem)
        def _(v):
            for j in range(tiles):
                cut = cut_all[v, j].astype(jnp.float32)
                misfit = 0.0 - both * image_all[v, j].astype(jnp.float32) - obs_all[v, j]
                sent_all[it, v, j] = jnp.minimum(jnp.maximum(misfit, -cut), cut).astype(
                    jnp.bfloat16
                )

    def rowcopy(src, dst_at, slot, side):
        target = me_r + 1 if side == 0 else me_r - 1
        return pltpu.make_async_remote_copy(
            src_ref=src, dst_ref=dst_at(side), send_sem=halo_send.at[slot, side],
            recv_sem=halo_recv.at[slot, side], device_id=to(me_m, target), device_id_type=MESH,
        )

    def row_start(src, dst_at, slot):
        @pl.when(has_high)
        def _():
            rowcopy(src, dst_at, slot, 0).start()

        @pl.when(has_low)
        def _():
            rowcopy(src, dst_at, slot, 1).start()

    def row_wait(src, dst_at, slot):
        @pl.when(has_low)
        def _():
            rowcopy(src, dst_at, slot, 0).wait_recv()

        @pl.when(has_high)
        def _():
            rowcopy(src, dst_at, slot, 1).wait_recv()

    def row_wait_send(src, dst_at, slot):
        @pl.when(has_high)
        def _():
            rowcopy(src, dst_at, slot, 0).wait_send()

        @pl.when(has_low)
        def _():
            rowcopy(src, dst_at, slot, 1).wait_send()

    n_slot = 3
    index_args = (send_index, lambda side: index_halo.at[side], ITERS * n_slot)

    def static_args(it):
        return send_static.at[it], lambda side: static_halo.at[it, side], it * n_slot

    def back_args(it, l):
        return send_back.at[it, l], lambda side: back_halo.at[it, side, l], it * n_slot + 1 + l

    def push(src, dst, send, recv, device):
        return pltpu.make_async_remote_copy(
            src_ref=src, dst_ref=dst, send_sem=send, recv_sem=recv,
            device_id=to(*device), device_id_type=MESH,
        )

    def gather_copy(ref, send, recv, d):
        return push(ref.at[me_m], ref.at[me_m], send, recv, device_at(*d))

    def part_copy(it, l, d):
        v, r = device_at(*d)
        return push(
            partial.at[it, l, v], arrived.at[it, l, me_m],
            part_send.at[it, l], part_recv.at[it, l], (v, r),
        )

    def first_copy(it, d):
        own = first.at[it, my_plane]
        return push(own, own, small_send.at[it, 0], small_recv.at[it, 0], device_at(*d))

    def second_copy(it, d):
        own = second.at[it, z]
        return push(own, own, small_send.at[it, 1], small_recv.at[it, 1], device_at(*d))

    across = (0, 0, 4, 0)
    partner = lax.rem(me_m + 4, 8)
    along_y = [(0, dy, 0, 0) for dy in (2, 1, 3)]

    def obs_across():
        return [
            push(ref.at[me_m], ref.at[me_m], obs_send.at[i], obs_recv.at[i], device_at(*across))
            for i, ref in enumerate((obs_all, cut_all))
        ]

    def obs_along(i, ref, slot, k):
        return [
            push(
                ref.at[slot], ref.at[slot], obs_send.at[2 + 2 * i + k],
                obs_recv.at[2 + 2 * i + k], device_at(*d),
            )
            for d in along_y
        ]

    def bytes_wait(ref, count, sem):
        part = ref.at[pl.ds(0, count)]
        pltpu.make_async_copy(part, part, sem).wait()

    def diffuse(it, l, g):
        low_in = jnp.where(has_low, 1.0, 0.0).astype(jnp.float32)
        high_in = jnp.where(has_high, 1.0, 0.0).astype(jnp.float32)
        for sweep in range(SWEEPS):
            lo, hi = sweep, 3 * rows - sweep

            def get(row):
                u = field[l, row, g]
                return u, u * kwide[l, row]

            _, w_prev = get(lo)
            u_cur, w_cur = get(lo + 1)
            norm = jnp.zeros((8, LANES), jnp.float32)
            for row in range(lo + 1, hi - 1):
                u_next, w_next = get(row + 1)
                out = (w_prev + w_next) + sideways(w_cur) + (u_cur - 4.0 * w_cur)
                if sweep < SWEEPS - 1:
                    field[l, row, g] = out
                else:
                    if it > 0:
                        out = out - step_ref[...] * grad[0, l, row - SWEEPS, g]
                    if row < rows:
                        out = out * low_in
                    elif row >= 2 * rows:
                        out = out * high_in
                    else:
                        norm = norm + jnp.sum(out * out, axis=0)
                    grad[it, l, row - SWEEPS, g] = out
                w_prev, u_cur, w_cur = w_cur, u_next, w_next
        norm_acc[...] += norm
        for sweep in range(SWEEPS):
            lo, hi = SWEEPS + sweep, 3 * rows - SWEEPS - sweep

            def load(row):
                return grad[it, l, row - SWEEPS, g] if sweep == 0 else field[l, row, g]

            u_prev, u_cur = load(lo), load(lo + 1)
            for row in range(lo + 1, hi - 1):
                u_next = load(row + 1)
                out = u_cur + kwide[l, row] * ((u_prev + u_next) + sideways(u_cur) - 4.0 * u_cur)
                if sweep < SWEEPS - 1:
                    field[l, row, g] = out
                else:
                    out = out.astype(jnp.bfloat16).astype(jnp.float32)
                    for j in range(tiles):
                        spread[l, j, pl.ds((row - rows) * 16 + g * 8, 8), :] = out[j]
                u_prev, u_cur = u_cur, u_next

    def diffuse_static(it, l):
        halo = static_halo[it].astype(jnp.float32)
        here = slice(l * rows, (l + 1) * rows)
        u = jnp.concatenate([halo[0, :, here], stat_back[l], halo[1, :, here]], 1)
        k = knat[l]
        grow = me_r * rows - rows + lax.broadcasted_iota(jnp.int32, (3 * rows, LANES), 0)
        inside = jnp.logical_and(grow >= 0, grow < n_row * rows)[None]
        n = 3 * rows
        for sweep in range(SWEEPS):
            w = k * u
            u = (pltpu.roll(w, 1, 1) + pltpu.roll(w, n - 1, 1)) + sideways(w) + (u - 4.0 * w)
        if it > 0:
            u = u - step_ref[:1] * stat_grad[0, l]
        u = jnp.where(inside, u, 0.0)
        stat_grad[it, l] = u
        own = u[:, rows:2 * rows]
        norm_acc[...] += jnp.sum(own * own, axis=0)
        for sweep in range(SWEEPS):
            u = u + k * (
                (pltpu.roll(u, 1, 1) + pltpu.roll(u, n - 1, 1)) + sideways(u) - 4.0 * u
            )
        for j in range(tiles):
            stat_part[l, j] = STAT * lane_tile(scale, l, j) * u[j, rows:2 * rows]

    first_sent()
    static_source(0)

    @pl.when(has_far)
    def _():
        pl.semaphore_wait(barrier, len(greeted) + 1)

    @pl.when(jnp.logical_not(has_far))
    def _():
        pl.semaphore_wait(barrier, len(greeted))

    for it in range(ITERS):
        if it == 0:
            for d in same_rows:
                gather_copy(sent_all.at[0], sent_send, sent_recv, d).start()
            row_start(*index_args)
        row_start(*static_args(it))
        if it == 0:
            for copy in obs_across():
                copy.start()
            for i, ref in enumerate((obs_all, cut_all)):
                for copy in obs_along(i, ref, me_m, 0):
                    copy.start()
        norm_acc[...] = jnp.zeros_like(norm_acc)
        if it == 0:
            row_wait(*index_args)
            for j in range(tiles):
                for l in range(2):
                    here = slice(l * rows, (l + 1) * rows)
                    both = index_halo[:, j].astype(jnp.float32)
                    ids = jnp.concatenate(
                        [both[0, here], lane_tile(index, l, j).astype(jnp.float32), both[1, here]],
                        0,
                    )
                    k = jnp.zeros_like(ids)
                    for i, value in enumerate(KAPPAS):
                        k = jnp.where(ids == i, value, k)
                    knat[l, j] = k
                    for row in range(3 * rows):
                        kwide[l, row, j] = jnp.broadcast_to(k[row:row + 1], (8, LANES))
            for load in loads[4:]:
                load.wait()
            bytes_wait(sent_all.at[0], n_mem - 1, sent_recv)

        @pl.loop(0, tiles)
        def _(j):
            wide = [sent_all[it, v, j].astype(jnp.float32) for v in range(n_mem)]
            for k in range(16):
                total = members[j, k, 0].astype(jnp.float32) * wide[0]
                for v in range(1, n_mem):
                    total = total + members[j, k, v].astype(jnp.float32) * wide[v]
                total = ens_coef * total
                for l in range(2):
                    turned[l, j, k * 8:(k + 1) * 8, :] = total[l * rows:(l + 1) * rows]

        for l in range(2):
            @pl.loop(0, tiles)
            def _(j):
                for r in range(rows):
                    half = [turned[l, j, pl.ds(g * 64 + r, 8, stride=8), :] for g in range(2)]
                    for g in range(2):
                        field[l, rows + r, g, j] = half[g]
                    send_back[it, l, r, j] = jnp.concatenate(half, 0).astype(jnp.bfloat16)

            row_start(*back_args(it, l))

        if it == 0:
            for copy in obs_across():
                copy.wait_recv()
            for i, ref in enumerate((obs_all, cut_all)):
                for copy in obs_along(i, ref, partner, 1):
                    copy.start()
        row_wait(*static_args(it))
        for l in range(2):
            diffuse_static(it, l)

        for l in range(2):
            row_wait(*back_args(it, l))

            @pl.loop(0, rows)
            def _(r):
                for j in range(tiles):
                    for side in range(2):
                        value = back_halo[it, side, l, r, j].astype(jnp.float32)
                        for g in range(2):
                            field[l, side * 2 * rows + r, g, j] = value[g * 8:(g + 1) * 8]

            @pl.loop(0, 2)
            def _(g):
                diffuse(it, l, g)

            @pl.loop(0, tiles // 2)
            def _(jj):
                totals = []
                for half in range(2):
                    j = jj * 2 + half
                    total = [None] * n_mem
                    for k in range(16):
                        s = spread[l, j, pl.ds(k, 8, stride=16), :]
                        for v in range(n_mem):
                            m = members[j, k, v, l * rows:(l + 1) * rows, :].astype(jnp.float32)
                            total[v] = m * s if k == 0 else total[v] + m * s
                    totals.append(total)
                for v in range(n_mem):
                    partial[it, l, v, jj] = jnp.concatenate(
                        [totals[0][v], totals[1][v]], 0
                    ).astype(jnp.bfloat16)

            for d in same_rows:
                part_copy(it, l, d).start()
            arrived[it, l, me_m] = partial[it, l, me_m]

        curv = jnp.zeros((8, LANES), jnp.float32)
        for l in range(2):
            bytes_wait(arrived.at[it, l], n_mem - 1, part_recv.at[it, l])
            total = arrived[it, l, 0].astype(jnp.float32)
            for v in range(1, n_mem):
                total = total + arrived[it, l, v].astype(jnp.float32)
            for j in range(tiles):
                part = total[j // 2, (j % 2) * 8:(j % 2) * 8 + 8]
                img = ens_coef * part + stat_part[l, j]
                image[l, j] = img
                cut = cutoff(l, j)
                misfit = 0.0 - lane_tile(observed, l, j)
                if it > 0:
                    misfit = increment[l, j] + misfit
                weight = cut / jnp.maximum(jnp.abs(misfit), jnp.where(cut == 0.0, 1.0, cut))
                curv = curv + weight * img * img

        first[it, my_plane] = jnp.concatenate(
            [
                jnp.sum(norm_acc[...], axis=0, keepdims=True),
                jnp.sum(curv, axis=0, keepdims=True),
            ],
            1,
        )
        for d in planes:
            first_copy(it, d).start()
        if it == 0:
            for j in range(tiles):
                image_all[me_m, j] = jnp.concatenate([image[0, j], image[1, j]], 0).astype(
                    jnp.bfloat16
                )
            for d in same_rows:
                gather_copy(image_all, image_send, image_recv, d).start()
        bytes_wait(first.at[it], n_first - 1, small_recv.at[it, 0])
        second[it, z] = jnp.sum(first[it], axis=0)
        for d in along_z:
            second_copy(it, d).start()
        if it == 0:
            for i, ref in enumerate((obs_all, cut_all)):
                for k in range(2):
                    bytes_wait(ref, 3, obs_recv.at[2 + 2 * i + k])
            bytes_wait(image_all, n_mem - 1, image_recv)
        else:
            for n, out in enumerate((before_o, grad_o)):
                @pl.loop(0, tiles)
                def _(j):
                    for l in range(2):
                        for r in range(rows):
                            for g in range(2):
                                value = grad[n, l, SWEEPS + r, g, j]
                                if n == 0:
                                    value = 0.0 - step_ref[...] * value
                                spread[l, j, r * 16 + g * 8:r * 16 + g * 8 + 8, :] = value

                for j in range(tiles):
                    for l in range(2):
                        for k in range(16):
                            out[k, l, :, j * LANES:(j + 1) * LANES] = spread[
                                l, j, pl.ds(k, 8, stride=16), :
                            ]
            for l in range(2):
                for j in range(tiles):
                    lanes = slice(j * LANES, (j + 1) * LANES)
                    own = slice(rows, 2 * rows)
                    stat_before_o[l, :, lanes] = 0.0 - step_ref[...] * stat_grad[0, l, j, own]
                    stat_grad_o[l, :, lanes] = stat_grad[1, l, j, own]
                    inc_before_o[l, :, lanes] = increment[l, j]
                    image_o[l, :, lanes] = image[l, j]
        bytes_wait(second.at[it], n_second - 1, small_recv.at[it, 1])
        sums = jnp.sum(second[it], axis=0)
        norm = jnp.sum(sums[:, :LANES], axis=1, keepdims=True)
        curvature = jnp.sum(sums[:, LANES:], axis=1, keepdims=True)
        step = jnp.broadcast_to(norm / (norm + curvature), (8, LANES))
        if it == 0:
            step_ref[...] = step
            next_sent(1, step)
            static_source(1)
            increment[...] = 0.0 - step * image[...]
        else:
            step_o[...] = step

    row_wait_send(*index_args)
    bytes_wait(sent_all.at[0], n_mem - 1, sent_send)
    bytes_wait(image_all, n_mem - 1, image_send)
    for copy in obs_across():
        copy.wait_send()
    for i, ref in enumerate((obs_all, cut_all)):
        for k in range(2):
            bytes_wait(ref, 3, obs_send.at[2 + 2 * i + k])
    for it in range(ITERS):
        row_wait_send(*static_args(it))
        for l in range(2):
            row_wait_send(*back_args(it, l))
            bytes_wait(arrived.at[it, l], n_mem - 1, part_send.at[it, l])
        bytes_wait(first.at[it], n_first - 1, small_send.at[it, 0])
        bytes_wait(second.at[it], n_second - 1, small_send.at[it, 1])


def local(n_mem, n_row, members, static_scale, observed, huber_class, scale_index):
    k, v, _, rows, cells = members.shape
    ens_coef = math.sqrt(0.7 / (k * n_mem - 1))
    f32, bf16 = jnp.float32, jnp.bfloat16
    tiles = cells // LANES
    V = pltpu.VMEM
    scratch = [
        V((tiles, k, v, 16, LANES), bf16),
        V((2, rows, cells), f32),
        V((2, rows, cells), f32),
        V((2, rows, cells), jnp.int32),
        V((2, rows, cells), jnp.int32),
        V((ITERS, n_mem, tiles, 16, LANES), bf16),
        V((ITERS, tiles, 16, LANES), bf16),
        V((ITERS, 2, tiles, 16, LANES), bf16),
        V((tiles, 16, LANES), bf16),
        V((2, tiles, 16, LANES), bf16),
        V((n_mem, tiles, 16, LANES), f32),
        V((n_mem, tiles, 16, LANES), bf16),
        V((n_mem, tiles, 16, LANES), bf16),
        V((2, 3 * rows, tiles, 8, LANES), f32),
        V((2, tiles, 3 * rows, LANES), f32),
        V((2, tiles, k * rows, LANES), f32),
        V((2, 3 * rows, 2, tiles, 8, LANES), f32),
        V((ITERS, 2, rows, tiles, 16, LANES), bf16),
        V((ITERS, 2, 2, rows, tiles, 16, LANES), bf16),
        V((ITERS, 2, 2 * rows, 2, tiles, 8, LANES), f32),
        V((2, tiles, k * rows, LANES), f32),
        V((ITERS, 2, n_mem, tiles // 2, 16, LANES), bf16),
        V((ITERS, 2, n_mem, tiles // 2, 16, LANES), bf16),
        V((ITERS, 2, tiles, 3 * rows, LANES), f32),
        V((2, tiles, rows, LANES), f32),
        V((2, tiles, rows, LANES), f32),
        V((2, tiles, rows, LANES), f32),
        V((2, tiles, rows, LANES), f32),
        V((8, LANES), f32),
        V((8, LANES), f32),
        V((ITERS, 32, 1, 2 * LANES), f32),
        V((ITERS, 8, 1, 2 * LANES), f32),
        pltpu.SemaphoreType.DMA((4 + tiles,)),
        pltpu.SemaphoreType.DMA,
        pltpu.SemaphoreType.DMA,
        pltpu.SemaphoreType.DMA((ITERS * 3 + 1, 2)),
        pltpu.SemaphoreType.DMA((ITERS * 3 + 1, 2)),
        pltpu.SemaphoreType.DMA((ITERS, 2)),
        pltpu.SemaphoreType.DMA((ITERS, 2)),
        pltpu.SemaphoreType.DMA((ITERS, 2)),
        pltpu.SemaphoreType.DMA((ITERS, 2)),
        pltpu.SemaphoreType.DMA((6,)),
        pltpu.SemaphoreType.DMA((6,)),
        pltpu.SemaphoreType.DMA,
        pltpu.SemaphoreType.DMA,
    ]
    hbm = pl.BlockSpec(memory_space=pltpu.HBM)
    vmem = pl.BlockSpec(memory_space=pltpu.VMEM)
    wide = jax.ShapeDtypeStruct((k, 2, rows, cells), f32)
    thin = jax.ShapeDtypeStruct((2, rows, cells), f32)
    state = pl.pallas_call(
        functools.partial(kernel, n_mem, n_row, ens_coef),
        out_shape=[wide, wide, thin, thin, thin, thin, jax.ShapeDtypeStruct((8, LANES), f32)],
        in_specs=[hbm] * 5,
        out_specs=[vmem] * 7,
        scratch_shapes=scratch,
        compiler_params=pltpu.CompilerParams(
            collective_id=0, has_side_effects=True, vmem_limit_bytes=60 * 1024 * 1024
        ),
    )(
        members.reshape(k, v, 2 * rows, cells),
        static_scale[0],
        observed[0],
        huber_class[0],
        scale_index,
    )
    before, grad, stat_before, stat_grad, inc_before, image, step = state
    step = step[0, 0]
    return (
        before - step * grad,
        (stat_before - step * stat_grad)[None],
        (inc_before - step * image)[None],
    )


def solution(mesh):
    sizes = dict(mesh.shape)
    placed = (
        P("mem", None, None, "row", None),
        P("mem", None, "row", None),
        P("mem", None, "row", None),
        P("mem", None, "row", None),
        P(None, "row", None),
    )
    return jax.shard_map(
        functools.partial(local, sizes["mem"], sizes["row"]),
        mesh=mesh,
        in_specs=placed,
        out_specs=(P("mem", None, "row", None),) * 3,
        check_vma=False,
    )
```

```python
import functools
import math

import jax
import jax.numpy as jnp
from jax import lax
from jax.experimental import pallas as pl
from jax.experimental.pallas import tpu as pltpu
from jax.sharding import PartitionSpec as P

SWEEPS = 4
ITERS = 2
KAPPAS = (0.06, 0.11, 0.17, 0.23)
LANES = 128
STAT = math.sqrt(0.3)
MESH = pl.DeviceIdType.MESH


def sideways(w):
    lane = lax.broadcasted_iota(jnp.int32, w.shape[1:], 1)[None]
    edge = jnp.zeros_like(w[:1])
    right = pltpu.roll(w, 1, 2)
    left = pltpu.roll(w, LANES - 1, 2)
    from_left = jnp.where(lane == 0, jnp.concatenate([edge, right[:-1]], 0), right)
    from_right = jnp.where(lane == LANES - 1, jnp.concatenate([left[1:], edge], 0), left)
    return from_left + from_right


def kernel(
    n_mem, n_row, ens_coef,
    members_h, scale_h, observed_h, huber_h, index_h,
    before_o, grad_o, stat_before_o, stat_grad_o, inc_before_o, image_o, step_o,
    members, scale, observed, huber, index,
    sent_all, send_static, static_halo, send_index, index_halo,
    obs_all, cut_all, image_all,
    kwide, knat, turned, field, send_back, back_halo,
    grad, spread, partial, arrived,
    stat_grad, stat_back, stat_part, image, increment, norm_acc, step_ref, first, second,
    load_sem, sent_send, sent_recv, halo_send, halo_recv, part_send, part_recv,
    small_send, small_recv, obs_send, obs_recv, image_send, image_recv,
):
    me_m = lax.axis_index("mem")
    me_r = lax.axis_index("row")
    rows = 8
    tiles = 4
    has_low = me_r > 0
    has_high = me_r < n_row - 1

    def to(m, r):
        return {"mem": m, "row": r}

    loads = [
        pltpu.make_async_copy(observed_h, observed, load_sem.at[0]),
        pltpu.make_async_copy(huber_h, huber, load_sem.at[1]),
        pltpu.make_async_copy(index_h, index, load_sem.at[2]),
        pltpu.make_async_copy(scale_h, scale, load_sem.at[3]),
    ] + [
        pltpu.make_async_copy(
            members_h.at[:, :, :, pl.ds(j * LANES, LANES)], members.at[j], load_sem.at[4 + j]
        )
        for j in range(tiles)
    ]
    for load in loads:
        load.start()

    z_hi, y = me_m // 4, lax.rem(me_m, 4)
    x, z_lo, core = me_r // 8, lax.rem(me_r // 2, 4), lax.rem(me_r, 2)
    z = z_hi * 4 + z_lo

    def device_at(dx, dy, dz, dc):
        zz = lax.rem(z + dz, 8)
        m = (zz // 4) * 4 + lax.rem(y + dy, 4)
        r = lax.rem(x + dx, 4) * 8 + lax.rem(zz, 4) * 2 + lax.rem(core + dc, 2)
        return m, r

    def hops(d):
        return -(min(d[0], 4 - d[0]) + min(d[1], 4 - d[1]) + min(d[2], 8 - d[2]))

    planes = [(dx, dy, 0, dc) for dx in range(4) for dy in range(4) for dc in range(2)]
    planes = sorted(planes[1:], key=hops)
    along_z = sorted([(0, 0, dz, 0) for dz in range(1, 8)], key=hops)
    same_rows = sorted([(0, dy, dz, 0) for dz in (0, 4) for dy in range(4)][1:], key=hops)
    my_plane = (x * 4 + y) * 2 + core
    n_first, n_second = 32, 8

    greeted = sorted(set(planes + along_z + same_rows), key=hops)
    barrier = pltpu.get_barrier_semaphore()
    for d in greeted:
        pl.semaphore_signal(barrier, inc=1, device_id=to(*device_at(*d)), device_id_type=MESH)
    far = jnp.where(core == 0, me_r - 1, me_r + 1)
    has_far = jnp.logical_and(far >= 0, far < n_row)

    @pl.when(has_far)
    def _():
        pl.semaphore_signal(barrier, inc=1, device_id=to(me_m, far), device_id_type=MESH)

    def lane_tile(ref, l, j):
        return ref[l, :, j * LANES:(j + 1) * LANES]

    def cutoff(l, j):
        h = lane_tile(huber, l, j)
        return jnp.where(h == 1, 0.5, jnp.where(h == 2, 1.0, jnp.where(h == 3, 2.0, 0.0))).astype(
            jnp.float32
        )

    for load in loads[:4]:
        load.wait()
    for j in range(tiles):
        send_index[j] = jnp.concatenate(
            [lane_tile(index, 0, j), lane_tile(index, 1, j)], 0
        ).astype(jnp.float32).astype(jnp.bfloat16)

    @pl.when(jnp.logical_not(has_low))
    def _():
        index_halo[0] = jnp.full(index_halo.shape[1:], -1.0, jnp.bfloat16)
        static_halo[:, 0] = jnp.zeros_like(static_halo[:, 0])
        for it in range(ITERS):
            for l in range(2):
                back_halo[it, 0, l] = jnp.zeros_like(back_halo[it, 0, l])

    @pl.when(jnp.logical_not(has_high))
    def _():
        index_halo[1] = jnp.full(index_halo.shape[1:], -1.0, jnp.bfloat16)
        static_halo[:, 1] = jnp.zeros_like(static_halo[:, 1])
        for it in range(ITERS):
            for l in range(2):
                back_halo[it, 1, l] = jnp.zeros_like(back_halo[it, 1, l])

    def static_source(it):
        for j in range(tiles):
            wide = sent_all[it, me_m, j].astype(jnp.float32)
            for l in range(2):
                stat_back[l, j] = STAT * lane_tile(scale, l, j) * wide[l * rows:(l + 1) * rows]
            send_static[it, j] = jnp.concatenate(
                [stat_back[0, j], stat_back[1, j]], 0
            ).astype(jnp.bfloat16)

    def first_sent():
        for j in range(tiles):
            cut = jnp.concatenate([cutoff(0, j), cutoff(1, j)], 0)
            seen = jnp.concatenate([lane_tile(observed, 0, j), lane_tile(observed, 1, j)], 0)
            obs_all[me_m, j] = seen
            cut_all[me_m, j] = cut.astype(jnp.bfloat16)
            sent_all[0, me_m, j] = jnp.minimum(jnp.maximum(0.0 - seen, -cut), cut).astype(
                jnp.bfloat16
            )

    def next_sent(it, step):
        both = jnp.concatenate([step, step], 0)

        @pl.loop(0, n_mem)
        def _(v):
            for j in range(tiles):
                cut = cut_all[v, j].astype(jnp.float32)
                misfit = 0.0 - both * image_all[v, j].astype(jnp.float32) - obs_all[v, j]
                sent_all[it, v, j] = jnp.minimum(jnp.maximum(misfit, -cut), cut).astype(
                    jnp.bfloat16
                )

    def rowcopy(src, dst_at, slot, side):
        target = me_r + 1 if side == 0 else me_r - 1
        return pltpu.make_async_remote_copy(
            src_ref=src, dst_ref=dst_at(side), send_sem=halo_send.at[slot, side],
            recv_sem=halo_recv.at[slot, side], device_id=to(me_m, target), device_id_type=MESH,
        )

    def row_start(src, dst_at, slot):
        @pl.when(has_high)
        def _():
            rowcopy(src, dst_at, slot, 0).start()

        @pl.when(has_low)
        def _():
            rowcopy(src, dst_at, slot, 1).start()

    def row_wait(src, dst_at, slot):
        @pl.when(has_low)
        def _():
            rowcopy(src, dst_at, slot, 0).wait_recv()

        @pl.when(has_high)
        def _():
            rowcopy(src, dst_at, slot, 1).wait_recv()

    def row_wait_send(src, dst_at, slot):
        @pl.when(has_high)
        def _():
            rowcopy(src, dst_at, slot, 0).wait_send()

        @pl.when(has_low)
        def _():
            rowcopy(src, dst_at, slot, 1).wait_send()

    n_slot = 3
    index_args = (send_index, lambda side: index_halo.at[side], ITERS * n_slot)

    def static_args(it):
        return send_static.at[it], lambda side: static_halo.at[it, side], it * n_slot

    def back_args(it, l):
        return send_back.at[it, l], lambda side: back_halo.at[it, side, l], it * n_slot + 1 + l

    def push(src, dst, send, recv, device):
        return pltpu.make_async_remote_copy(
            src_ref=src, dst_ref=dst, send_sem=send, recv_sem=recv,
            device_id=to(*device), device_id_type=MESH,
        )

    def gather_copy(ref, send, recv, d):
        return push(ref.at[me_m], ref.at[me_m], send, recv, device_at(*d))

    def part_copy(it, l, d):
        v, r = device_at(*d)
        return push(
            partial.at[it, l, v], arrived.at[it, l, me_m],
            part_send.at[it, l], part_recv.at[it, l], (v, r),
        )

    def first_copy(it, d):
        own = first.at[it, my_plane]
        return push(own, own, small_send.at[it, 0], small_recv.at[it, 0], device_at(*d))

    def second_copy(it, d):
        own = second.at[it, z]
        return push(own, own, small_send.at[it, 1], small_recv.at[it, 1], device_at(*d))

    across = (0, 0, 4, 0)
    partner = lax.rem(me_m + 4, 8)
    along_y = [(0, dy, 0, 0) for dy in (2, 1, 3)]

    def obs_across():
        return [
            push(ref.at[me_m], ref.at[me_m], obs_send.at[i], obs_recv.at[i], device_at(*across))
            for i, ref in enumerate((obs_all, cut_all))
        ]

    def obs_along(i, ref, slot, k):
        return [
            push(
                ref.at[slot], ref.at[slot], obs_send.at[2 + 2 * i + k],
                obs_recv.at[2 + 2 * i + k], device_at(*d),
            )
            for d in along_y
        ]

    def bytes_wait(ref, count, sem):
        part = ref.at[pl.ds(0, count)]
        pltpu.make_async_copy(part, part, sem).wait()

    def diffuse(it, l, g):
        low_in = jnp.where(has_low, 1.0, 0.0).astype(jnp.float32)
        high_in = jnp.where(has_high, 1.0, 0.0).astype(jnp.float32)
        for sweep in range(SWEEPS):
            lo, hi = sweep, 3 * rows - sweep

            def get(row):
                u = field[l, row, g]
                return u, u * kwide[l, row]

            _, w_prev = get(lo)
            u_cur, w_cur = get(lo + 1)
            norm = jnp.zeros((8, LANES), jnp.float32)
            for row in range(lo + 1, hi - 1):
                u_next, w_next = get(row + 1)
                out = (w_prev + w_next) + sideways(w_cur) + (u_cur - 4.0 * w_cur)
                if sweep < SWEEPS - 1:
                    field[l, row, g] = out
                else:
                    if it > 0:
                        out = out - step_ref[...] * grad[0, l, row - SWEEPS, g]
                    if row < rows:
                        out = out * low_in
                    elif row >= 2 * rows:
                        out = out * high_in
                    else:
                        norm = norm + jnp.sum(out * out, axis=0)
                    grad[it, l, row - SWEEPS, g] = out
                w_prev, u_cur, w_cur = w_cur, u_next, w_next
        norm_acc[...] += norm
        for sweep in range(SWEEPS):
            lo, hi = SWEEPS + sweep, 3 * rows - SWEEPS - sweep

            def load(row):
                return grad[it, l, row - SWEEPS, g] if sweep == 0 else field[l, row, g]

            u_prev, u_cur = load(lo), load(lo + 1)
            for row in range(lo + 1, hi - 1):
                u_next = load(row + 1)
                out = u_cur + kwide[l, row] * ((u_prev + u_next) + sideways(u_cur) - 4.0 * u_cur)
                if sweep < SWEEPS - 1:
                    field[l, row, g] = out
                else:
                    out = out.astype(jnp.bfloat16).astype(jnp.float32)
                    for j in range(tiles):
                        spread[l, j, pl.ds((row - rows) * 16 + g * 8, 8), :] = out[j]
                u_prev, u_cur = u_cur, u_next

    def diffuse_static(it, l):
        halo = static_halo[it].astype(jnp.float32)
        here = slice(l * rows, (l + 1) * rows)
        u = jnp.concatenate([halo[0, :, here], stat_back[l], halo[1, :, here]], 1)
        k = knat[l]
        grow = me_r * rows - rows + lax.broadcasted_iota(jnp.int32, (3 * rows, LANES), 0)
        inside = jnp.logical_and(grow >= 0, grow < n_row * rows)[None]
        n = 3 * rows
        for sweep in range(SWEEPS):
            w = k * u
            u = (pltpu.roll(w, 1, 1) + pltpu.roll(w, n - 1, 1)) + sideways(w) + (u - 4.0 * w)
        if it > 0:
            u = u - step_ref[:1] * stat_grad[0, l]
        u = jnp.where(inside, u, 0.0)
        stat_grad[it, l] = u
        own = u[:, rows:2 * rows]
        norm_acc[...] += jnp.sum(own * own, axis=0)
        for sweep in range(SWEEPS):
            u = u + k * (
                (pltpu.roll(u, 1, 1) + pltpu.roll(u, n - 1, 1)) + sideways(u) - 4.0 * u
            )
        for j in range(tiles):
            stat_part[l, j] = STAT * lane_tile(scale, l, j) * u[j, rows:2 * rows]

    first_sent()
    static_source(0)

    @pl.when(has_far)
    def _():
        pl.semaphore_wait(barrier, len(greeted) + 1)

    @pl.when(jnp.logical_not(has_far))
    def _():
        pl.semaphore_wait(barrier, len(greeted))

    for it in range(ITERS):
        if it == 0:
            for d in same_rows:
                gather_copy(sent_all.at[0], sent_send, sent_recv, d).start()
            row_start(*index_args)
        row_start(*static_args(it))
        if it == 0:
            for copy in obs_across():
                copy.start()
            for i, ref in enumerate((obs_all, cut_all)):
                for copy in obs_along(i, ref, me_m, 0):
                    copy.start()
        norm_acc[...] = jnp.zeros_like(norm_acc)
        if it == 0:
            row_wait(*index_args)
            for j in range(tiles):
                for l in range(2):
                    here = slice(l * rows, (l + 1) * rows)
                    both = index_halo[:, j].astype(jnp.float32)
                    ids = jnp.concatenate(
                        [both[0, here], lane_tile(index, l, j).astype(jnp.float32), both[1, here]],
                        0,
                    )
                    k = jnp.zeros_like(ids)
                    for i, value in enumerate(KAPPAS):
                        k = jnp.where(ids == i, value, k)
                    knat[l, j] = k
                    for row in range(3 * rows):
                        kwide[l, row, j] = jnp.broadcast_to(k[row:row + 1], (8, LANES))
            for load in loads[4:]:
                load.wait()
            bytes_wait(sent_all.at[0], n_mem - 1, sent_recv)

        @pl.loop(0, tiles)
        def _(j):
            wide = [sent_all[it, v, j].astype(jnp.float32) for v in range(n_mem)]
            for k in range(16):
                total = members[j, k, 0].astype(jnp.float32) * wide[0]
                for v in range(1, n_mem):
                    total = total + members[j, k, v].astype(jnp.float32) * wide[v]
                total = ens_coef * total
                for l in range(2):
                    turned[l, j, k * 8:(k + 1) * 8, :] = total[l * rows:(l + 1) * rows]

        for l in range(2):
            @pl.loop(0, tiles)
            def _(j):
                for r in range(rows):
                    half = [turned[l, j, pl.ds(g * 64 + r, 8, stride=8), :] for g in range(2)]
                    for g in range(2):
                        field[l, rows + r, g, j] = half[g]
                    send_back[it, l, r, j] = jnp.concatenate(half, 0).astype(jnp.bfloat16)

            row_start(*back_args(it, l))

        if it == 0:
            for copy in obs_across():
                copy.wait_recv()
            for i, ref in enumerate((obs_all, cut_all)):
                for copy in obs_along(i, ref, partner, 1):
                    copy.start()
        row_wait(*static_args(it))
        for l in range(2):
            diffuse_static(it, l)

        for l in range(2):
            row_wait(*back_args(it, l))

            @pl.loop(0, rows)
            def _(r):
                for j in range(tiles):
                    for side in range(2):
                        value = back_halo[it, side, l, r, j].astype(jnp.float32)
                        for g in range(2):
                            field[l, side * 2 * rows + r, g, j] = value[g * 8:(g + 1) * 8]

            @pl.loop(0, 2)
            def _(g):
                diffuse(it, l, g)

            @pl.loop(0, tiles // 2)
            def _(jj):
                totals = []
                for half in range(2):
                    j = jj * 2 + half
                    total = [None] * n_mem
                    for k in range(16):
                        s = spread[l, j, pl.ds(k, 8, stride=16), :]
                        for v in range(n_mem):
                            m = members[j, k, v, l * rows:(l + 1) * rows, :].astype(jnp.float32)
                            total[v] = m * s if k == 0 else total[v] + m * s
                    totals.append(total)
                for v in range(n_mem):
                    partial[it, l, v, jj] = jnp.concatenate(
                        [totals[0][v], totals[1][v]], 0
                    ).astype(jnp.bfloat16)

            for d in same_rows:
                part_copy(it, l, d).start()
            arrived[it, l, me_m] = partial[it, l, me_m]

        curv = jnp.zeros((8, LANES), jnp.float32)
        for l in range(2):
            bytes_wait(arrived.at[it, l], n_mem - 1, part_recv.at[it, l])
            total = arrived[it, l, 0].astype(jnp.float32)
            for v in range(1, n_mem):
                total = total + arrived[it, l, v].astype(jnp.float32)
            for j in range(tiles):
                part = total[j // 2, (j % 2) * 8:(j % 2) * 8 + 8]
                img = ens_coef * part + stat_part[l, j]
                image[l, j] = img
                cut = cutoff(l, j)
                misfit = 0.0 - lane_tile(observed, l, j)
                if it > 0:
                    misfit = increment[l, j] + misfit
                weight = cut / jnp.maximum(jnp.abs(misfit), jnp.where(cut == 0.0, 1.0, cut))
                curv = curv + weight * img * img

        first[it, my_plane] = jnp.concatenate(
            [
                jnp.sum(norm_acc[...], axis=0, keepdims=True),
                jnp.sum(curv, axis=0, keepdims=True),
            ],
            1,
        )
        for d in planes:
            first_copy(it, d).start()
        if it == 0:
            for j in range(tiles):
                image_all[me_m, j] = jnp.concatenate([image[0, j], image[1, j]], 0).astype(
                    jnp.bfloat16
                )
            for d in same_rows:
                gather_copy(image_all, image_send, image_recv, d).start()
        bytes_wait(first.at[it], n_first - 1, small_recv.at[it, 0])
        second[it, z] = jnp.sum(first[it], axis=0)
        for d in along_z:
            second_copy(it, d).start()
        if it == 0:
            for i, ref in enumerate((obs_all, cut_all)):
                for k in range(2):
                    bytes_wait(ref, 3, obs_recv.at[2 + 2 * i + k])
            bytes_wait(image_all, n_mem - 1, image_recv)
        else:
            for n, out in enumerate((before_o, grad_o)):
                @pl.loop(0, tiles)
                def _(j):
                    for l in range(2):
                        for r in range(rows):
                            for g in range(2):
                                value = grad[n, l, SWEEPS + r, g, j]
                                if n == 0:
                                    value = 0.0 - step_ref[...] * value
                                spread[l, j, r * 16 + g * 8:r * 16 + g * 8 + 8, :] = value

                for j in range(tiles):
                    for l in range(2):
                        for k in range(16):
                            out[k, l, :, j * LANES:(j + 1) * LANES] = spread[
                                l, j, pl.ds(k, 8, stride=16), :
                            ]
            for l in range(2):
                for j in range(tiles):
                    lanes = slice(j * LANES, (j + 1) * LANES)
                    own = slice(rows, 2 * rows)
                    stat_before_o[l, :, lanes] = 0.0 - step_ref[...] * stat_grad[0, l, j, own]
                    stat_grad_o[l, :, lanes] = stat_grad[1, l, j, own]
                    inc_before_o[l, :, lanes] = increment[l, j]
                    image_o[l, :, lanes] = image[l, j]
        bytes_wait(second.at[it], n_second - 1, small_recv.at[it, 1])
        sums = jnp.sum(second[it], axis=0)
        norm = jnp.sum(sums[:, :LANES], axis=1, keepdims=True)
        curvature = jnp.sum(sums[:, LANES:], axis=1, keepdims=True)
        step = jnp.broadcast_to(norm / (norm + curvature), (8, LANES))
        if it == 0:
            step_ref[...] = step
            next_sent(1, step)
            static_source(1)
            increment[...] = 0.0 - step * image[...]
        else:
            step_o[...] = step

    row_wait_send(*index_args)
    bytes_wait(sent_all.at[0], n_mem - 1, sent_send)
    bytes_wait(image_all, n_mem - 1, image_send)
    for copy in obs_across():
        copy.wait_send()
    for i, ref in enumerate((obs_all, cut_all)):
        for k in range(2):
            bytes_wait(ref, 3, obs_send.at[2 + 2 * i + k])
    for it in range(ITERS):
        row_wait_send(*static_args(it))
        for l in range(2):
            row_wait_send(*back_args(it, l))
            bytes_wait(arrived.at[it, l], n_mem - 1, part_send.at[it, l])
        bytes_wait(first.at[it], n_first - 1, small_send.at[it, 0])
        bytes_wait(second.at[it], n_second - 1, small_send.at[it, 1])


def local(n_mem, n_row, members, static_scale, observed, huber_class, scale_index):
    k, v, _, rows, cells = members.shape
    ens_coef = math.sqrt(0.7 / (k * n_mem - 1))
    f32, bf16 = jnp.float32, jnp.bfloat16
    tiles = cells // LANES
    V = pltpu.VMEM
    scratch = [
        V((tiles, k, v, 16, LANES), bf16),
        V((2, rows, cells), f32),
        V((2, rows, cells), f32),
        V((2, rows, cells), jnp.int32),
        V((2, rows, cells), jnp.int32),
        V((ITERS, n_mem, tiles, 16, LANES), bf16),
        V((ITERS, tiles, 16, LANES), bf16),
        V((ITERS, 2, tiles, 16, LANES), bf16),
        V((tiles, 16, LANES), bf16),
        V((2, tiles, 16, LANES), bf16),
        V((n_mem, tiles, 16, LANES), f32),
        V((n_mem, tiles, 16, LANES), bf16),
        V((n_mem, tiles, 16, LANES), bf16),
        V((2, 3 * rows, tiles, 8, LANES), f32),
        V((2, tiles, 3 * rows, LANES), f32),
        V((2, tiles, k * rows, LANES), f32),
        V((2, 3 * rows, 2, tiles, 8, LANES), f32),
        V((ITERS, 2, rows, tiles, 16, LANES), bf16),
        V((ITERS, 2, 2, rows, tiles, 16, LANES), bf16),
        V((ITERS, 2, 2 * rows, 2, tiles, 8, LANES), f32),
        V((2, tiles, k * rows, LANES), f32),
        V((ITERS, 2, n_mem, tiles // 2, 16, LANES), bf16),
        V((ITERS, 2, n_mem, tiles // 2, 16, LANES), bf16),
        V((ITERS, 2, tiles, 3 * rows, LANES), f32),
        V((2, tiles, rows, LANES), f32),
        V((2, tiles, rows, LANES), f32),
        V((2, tiles, rows, LANES), f32),
        V((2, tiles, rows, LANES), f32),
        V((8, LANES), f32),
        V((8, LANES), f32),
        V((ITERS, 32, 1, 2 * LANES), f32),
        V((ITERS, 8, 1, 2 * LANES), f32),
        pltpu.SemaphoreType.DMA((4 + tiles,)),
        pltpu.SemaphoreType.DMA,
        pltpu.SemaphoreType.DMA,
        pltpu.SemaphoreType.DMA((ITERS * 3 + 1, 2)),
        pltpu.SemaphoreType.DMA((ITERS * 3 + 1, 2)),
        pltpu.SemaphoreType.DMA((ITERS, 2)),
        pltpu.SemaphoreType.DMA((ITERS, 2)),
        pltpu.SemaphoreType.DMA((ITERS, 2)),
        pltpu.SemaphoreType.DMA((ITERS, 2)),
        pltpu.SemaphoreType.DMA((6,)),
        pltpu.SemaphoreType.DMA((6,)),
        pltpu.SemaphoreType.DMA,
        pltpu.SemaphoreType.DMA,
    ]
    hbm = pl.BlockSpec(memory_space=pltpu.HBM)
    vmem = pl.BlockSpec(memory_space=pltpu.VMEM)
    wide = pltpu.VMEM((k, 2, rows, cells), f32)
    thin = pltpu.VMEM((2, rows, cells), f32)
    state = pl.pallas_call(
        functools.partial(kernel, n_mem, n_row, ens_coef),
        out_shape=[wide, wide, thin, thin, thin, thin, pltpu.VMEM((8, LANES), f32)],
        in_specs=[hbm] * 5,
        out_specs=[vmem] * 7,
        scratch_shapes=scratch,
        compiler_params=pltpu.CompilerParams(
            collective_id=0, has_side_effects=True, vmem_limit_bytes=60 * 1024 * 1024
        ),
    )(
        members.reshape(k, v, 2 * rows, cells),
        static_scale[0],
        observed[0],
        huber_class[0],
        scale_index,
    )
    before, grad, stat_before, stat_grad, inc_before, image, step = state
    step = step[0, 0]
    return (
        before - step * grad,
        (stat_before - step * stat_grad)[None],
        (inc_before - step * image)[None],
    )


def solution(mesh):
    sizes = dict(mesh.shape)
    placed = (
        P("mem", None, None, "row", None),
        P("mem", None, "row", None),
        P("mem", None, "row", None),
        P("mem", None, "row", None),
        P(None, "row", None),
    )
    return jax.shard_map(
        functools.partial(local, sizes["mem"], sizes["row"]),
        mesh=mesh,
        in_specs=placed,
        out_specs=(P("mem", None, "row", None),) * 3,
        check_vma=False,
    )
```

```python
import functools
import math

import jax
import jax.numpy as jnp
from jax import lax
from jax.experimental import pallas as pl
from jax.experimental.pallas import tpu as pltpu
from jax.sharding import PartitionSpec as P

SWEEPS = 4
ITERS = 2
KAPPAS = (0.06, 0.11, 0.17, 0.23)
LANES = 128
STAT = math.sqrt(0.3)
MESH = pl.DeviceIdType.MESH


def sideways(w):
    lane = lax.broadcasted_iota(jnp.int32, w.shape[1:], 1)[None]
    edge = jnp.zeros_like(w[:1])
    right = pltpu.roll(w, 1, 2)
    left = pltpu.roll(w, LANES - 1, 2)
    from_left = jnp.where(lane == 0, jnp.concatenate([edge, right[:-1]], 0), right)
    from_right = jnp.where(lane == LANES - 1, jnp.concatenate([left[1:], edge], 0), left)
    return from_left + from_right


def kernel(
    n_mem, n_row, ens_coef,
    members_h, scale_h, observed_h, huber_h, index_h,
    control_o, static_o, increment_o,
    members, scale, observed, huber, index,
    sent_all, send_static, static_halo, send_index, index_halo,
    obs_all, cut_all, image_all,
    kwide, knat, turned, field, send_back, back_halo,
    grad, spread, partial, arrived,
    stat_grad, stat_back, stat_part, image, increment, norm_acc, step_ref, first, second,
    load_sem, sent_send, sent_recv, halo_send, halo_recv, part_send, part_recv,
    grad_nat, small_send, small_recv, obs_send, obs_recv, image_send, image_recv,
):
    me_m = lax.axis_index("mem")
    me_r = lax.axis_index("row")
    rows = 8
    tiles = 4
    has_low = me_r > 0
    has_high = me_r < n_row - 1

    def to(m, r):
        return {"mem": m, "row": r}

    loads = [
        pltpu.make_async_copy(observed_h, observed, load_sem.at[0]),
        pltpu.make_async_copy(huber_h, huber, load_sem.at[1]),
        pltpu.make_async_copy(index_h, index, load_sem.at[2]),
        pltpu.make_async_copy(scale_h, scale, load_sem.at[3]),
    ] + [
        pltpu.make_async_copy(
            members_h.at[:, :, :, pl.ds(j * LANES, LANES)], members.at[j], load_sem.at[4 + j]
        )
        for j in range(tiles)
    ]
    for load in loads:
        load.start()

    z_hi, y = me_m // 4, lax.rem(me_m, 4)
    x, z_lo, core = me_r // 8, lax.rem(me_r // 2, 4), lax.rem(me_r, 2)
    z = z_hi * 4 + z_lo

    def device_at(dx, dy, dz, dc):
        zz = lax.rem(z + dz, 8)
        m = (zz // 4) * 4 + lax.rem(y + dy, 4)
        r = lax.rem(x + dx, 4) * 8 + lax.rem(zz, 4) * 2 + lax.rem(core + dc, 2)
        return m, r

    def hops(d):
        return -(min(d[0], 4 - d[0]) + min(d[1], 4 - d[1]) + min(d[2], 8 - d[2]))

    planes = [(dx, dy, 0, dc) for dx in range(4) for dy in range(4) for dc in range(2)]
    planes = sorted(planes[1:], key=hops)
    along_z = sorted([(0, 0, dz, 0) for dz in range(1, 8)], key=hops)
    same_rows = sorted([(0, dy, dz, 0) for dz in (0, 4) for dy in range(4)][1:], key=hops)
    my_plane = (x * 4 + y) * 2 + core
    n_first, n_second = 32, 8

    greeted = sorted(set(planes + along_z + same_rows), key=hops)
    barrier = pltpu.get_barrier_semaphore()
    for d in greeted:
        pl.semaphore_signal(barrier, inc=1, device_id=to(*device_at(*d)), device_id_type=MESH)
    far = jnp.where(core == 0, me_r - 1, me_r + 1)
    has_far = jnp.logical_and(far >= 0, far < n_row)

    @pl.when(has_far)
    def _():
        pl.semaphore_signal(barrier, inc=1, device_id=to(me_m, far), device_id_type=MESH)

    def lane_tile(ref, l, j):
        return ref[l, :, j * LANES:(j + 1) * LANES]

    def cutoff(l, j):
        h = lane_tile(huber, l, j)
        return jnp.where(h == 1, 0.5, jnp.where(h == 2, 1.0, jnp.where(h == 3, 2.0, 0.0))).astype(
            jnp.float32
        )

    for load in loads[:4]:
        load.wait()
    for j in range(tiles):
        send_index[j] = jnp.concatenate(
            [lane_tile(index, 0, j), lane_tile(index, 1, j)], 0
        ).astype(jnp.float32).astype(jnp.bfloat16)

    @pl.when(jnp.logical_not(has_low))
    def _():
        index_halo[0] = jnp.full(index_halo.shape[1:], -1.0, jnp.bfloat16)
        static_halo[:, 0] = jnp.zeros_like(static_halo[:, 0])
        for it in range(ITERS):
            for l in range(2):
                for g in range(2):
                    back_halo[it, 0, l, g] = jnp.zeros_like(back_halo[it, 0, l, g])

    @pl.when(jnp.logical_not(has_high))
    def _():
        index_halo[1] = jnp.full(index_halo.shape[1:], -1.0, jnp.bfloat16)
        static_halo[:, 1] = jnp.zeros_like(static_halo[:, 1])
        for it in range(ITERS):
            for l in range(2):
                for g in range(2):
                    back_halo[it, 1, l, g] = jnp.zeros_like(back_halo[it, 1, l, g])

    def static_source(it):
        for j in range(tiles):
            wide = sent_all[it, me_m, j].astype(jnp.float32)
            for l in range(2):
                stat_back[l, j] = STAT * lane_tile(scale, l, j) * wide[l * rows:(l + 1) * rows]
            send_static[it, j] = jnp.concatenate(
                [stat_back[0, j], stat_back[1, j]], 0
            ).astype(jnp.bfloat16)

    def first_sent():
        for j in range(tiles):
            cut = jnp.concatenate([cutoff(0, j), cutoff(1, j)], 0)
            seen = jnp.concatenate([lane_tile(observed, 0, j), lane_tile(observed, 1, j)], 0)
            obs_all[me_m, j] = seen
            cut_all[me_m, j] = cut.astype(jnp.bfloat16)
            sent_all[0, me_m, j] = jnp.minimum(jnp.maximum(0.0 - seen, -cut), cut).astype(
                jnp.bfloat16
            )

    def next_sent(it, step):
        both = jnp.concatenate([step, step], 0)

        @pl.loop(0, n_mem)
        def _(v):
            for j in range(tiles):
                cut = cut_all[v, j].astype(jnp.float32)
                misfit = 0.0 - both * image_all[v, j].astype(jnp.float32) - obs_all[v, j]
                sent_all[it, v, j] = jnp.minimum(jnp.maximum(misfit, -cut), cut).astype(
                    jnp.bfloat16
                )

    def rowcopy(src, dst_at, slot, side):
        target = me_r + 1 if side == 0 else me_r - 1
        return pltpu.make_async_remote_copy(
            src_ref=src, dst_ref=dst_at(side), send_sem=halo_send.at[slot, side],
            recv_sem=halo_recv.at[slot, side], device_id=to(me_m, target), device_id_type=MESH,
        )

    def row_start(src, dst_at, slot):
        @pl.when(has_high)
        def _():
            rowcopy(src, dst_at, slot, 0).start()

        @pl.when(has_low)
        def _():
            rowcopy(src, dst_at, slot, 1).start()

    def row_wait(src, dst_at, slot):
        @pl.when(has_low)
        def _():
            rowcopy(src, dst_at, slot, 0).wait_recv()

        @pl.when(has_high)
        def _():
            rowcopy(src, dst_at, slot, 1).wait_recv()

    def row_wait_send(src, dst_at, slot):
        @pl.when(has_high)
        def _():
            rowcopy(src, dst_at, slot, 0).wait_send()

        @pl.when(has_low)
        def _():
            rowcopy(src, dst_at, slot, 1).wait_send()

    n_slot = 5
    index_args = (send_index, lambda side: index_halo.at[side], ITERS * n_slot)

    def static_args(it):
        return send_static.at[it], lambda side: static_halo.at[it, side], it * n_slot

    def back_args(it, l, g):
        slot = it * n_slot + 1 + g * 2 + l
        return send_back.at[it, l, g], lambda side: back_halo.at[it, side, l, g], slot

    def push(src, dst, send, recv, device):
        return pltpu.make_async_remote_copy(
            src_ref=src, dst_ref=dst, send_sem=send, recv_sem=recv,
            device_id=to(*device), device_id_type=MESH,
        )

    def gather_copy(ref, send, recv, d):
        return push(ref.at[me_m], ref.at[me_m], send, recv, device_at(*d))

    def part_copy(it, l, d):
        v, r = device_at(*d)
        return push(
            partial.at[it, l, v], arrived.at[it, l, me_m],
            part_send.at[it, l], part_recv.at[it, l], (v, r),
        )

    def first_copy(it, d):
        own = first.at[it, my_plane]
        return push(own, own, small_send.at[it, 0], small_recv.at[it, 0], device_at(*d))

    def second_copy(it, d):
        own = second.at[it, z]
        return push(own, own, small_send.at[it, 1], small_recv.at[it, 1], device_at(*d))

    across = (0, 0, 4, 0)
    partner = lax.rem(me_m + 4, 8)
    along_y = [(0, dy, 0, 0) for dy in (2, 1, 3)]

    def obs_across():
        return [
            push(ref.at[me_m], ref.at[me_m], obs_send.at[i], obs_recv.at[i], device_at(*across))
            for i, ref in enumerate((obs_all, cut_all))
        ]

    def obs_along(i, ref, slot, k):
        return [
            push(
                ref.at[slot], ref.at[slot], obs_send.at[2 + 2 * i + k],
                obs_recv.at[2 + 2 * i + k], device_at(*d),
            )
            for d in along_y
        ]

    def bytes_wait(ref, count, sem):
        part = ref.at[pl.ds(0, count)]
        pltpu.make_async_copy(part, part, sem).wait()

    def diffuse(it, l, g):
        low_in = jnp.where(has_low, 1.0, 0.0).astype(jnp.float32)
        high_in = jnp.where(has_high, 1.0, 0.0).astype(jnp.float32)
        for sweep in range(SWEEPS):
            lo, hi = sweep, 3 * rows - sweep

            def get(row):
                u = field[l, row, g]
                return u, u * kwide[l, row]

            _, w_prev = get(lo)
            u_cur, w_cur = get(lo + 1)
            norm = jnp.zeros((8, LANES), jnp.float32)
            for row in range(lo + 1, hi - 1):
                u_next, w_next = get(row + 1)
                out = (w_prev + w_next) + sideways(w_cur) + (u_cur - 4.0 * w_cur)
                if sweep < SWEEPS - 1:
                    field[l, row, g] = out
                else:
                    if it > 0:
                        out = out - step_ref[...] * grad[0, l, row - SWEEPS, g]
                    if row < rows:
                        out = out * low_in
                    elif row >= 2 * rows:
                        out = out * high_in
                    else:
                        norm = norm + jnp.sum(out * out, axis=0)
                    grad[it, l, row - SWEEPS, g] = out
                w_prev, u_cur, w_cur = w_cur, u_next, w_next
        norm_acc[...] += norm
        for sweep in range(SWEEPS):
            lo, hi = SWEEPS + sweep, 3 * rows - SWEEPS - sweep

            def load(row):
                return grad[it, l, row - SWEEPS, g] if sweep == 0 else field[l, row, g]

            u_prev, u_cur = load(lo), load(lo + 1)
            for row in range(lo + 1, hi - 1):
                u_next = load(row + 1)
                out = u_cur + kwide[l, row] * ((u_prev + u_next) + sideways(u_cur) - 4.0 * u_cur)
                if sweep < SWEEPS - 1:
                    field[l, row, g] = out
                else:
                    out = out.astype(jnp.bfloat16).astype(jnp.float32)
                    for j in range(tiles):
                        spread[l, j, pl.ds((row - rows) * 16 + g * 8, 8), :] = out[j]
                u_prev, u_cur = u_cur, u_next

    def diffuse_static(it, l):
        halo = static_halo[it].astype(jnp.float32)
        here = slice(l * rows, (l + 1) * rows)
        u = jnp.concatenate([halo[0, :, here], stat_back[l], halo[1, :, here]], 1)
        k = knat[l]
        grow = me_r * rows - rows + lax.broadcasted_iota(jnp.int32, (3 * rows, LANES), 0)
        inside = jnp.logical_and(grow >= 0, grow < n_row * rows)[None]
        n = 3 * rows
        for sweep in range(SWEEPS):
            w = k * u
            u = (pltpu.roll(w, 1, 1) + pltpu.roll(w, n - 1, 1)) + sideways(w) + (u - 4.0 * w)
        if it > 0:
            u = u - step_ref[:1] * stat_grad[0, l]
        u = jnp.where(inside, u, 0.0)
        stat_grad[it, l] = u
        own = u[:, rows:2 * rows]
        norm_acc[...] += jnp.sum(own * own, axis=0)
        for sweep in range(SWEEPS):
            u = u + k * (
                (pltpu.roll(u, 1, 1) + pltpu.roll(u, n - 1, 1)) + sideways(u) - 4.0 * u
            )
        for j in range(tiles):
            stat_part[l, j] = STAT * lane_tile(scale, l, j) * u[j, rows:2 * rows]

    first_sent()
    static_source(0)

    @pl.when(has_far)
    def _():
        pl.semaphore_wait(barrier, len(greeted) + 1)

    @pl.when(jnp.logical_not(has_far))
    def _():
        pl.semaphore_wait(barrier, len(greeted))

    for it in range(ITERS):
        if it == 0:
            for d in same_rows:
                gather_copy(sent_all.at[0], sent_send, sent_recv, d).start()
            row_start(*index_args)
        row_start(*static_args(it))
        norm_acc[...] = jnp.zeros_like(norm_acc)
        if it == 0:
            row_wait(*index_args)
            for j in range(tiles):
                for l in range(2):
                    here = slice(l * rows, (l + 1) * rows)
                    both = index_halo[:, j].astype(jnp.float32)
                    ids = jnp.concatenate(
                        [both[0, here], lane_tile(index, l, j).astype(jnp.float32), both[1, here]],
                        0,
                    )
                    k = jnp.zeros_like(ids)
                    for i, value in enumerate(KAPPAS):
                        k = jnp.where(ids == i, value, k)
                    knat[l, j] = k
                    for row in range(3 * rows):
                        kwide[l, row, j] = jnp.broadcast_to(k[row:row + 1], (8, LANES))
            for load in loads[4:]:
                load.wait()
            bytes_wait(sent_all.at[0], n_mem - 1, sent_recv)

        for g in range(2):
            @pl.loop(0, tiles)
            def _(j):
                wide = [sent_all[it, v, j].astype(jnp.float32) for v in range(n_mem)]
                for k in range(g * 8, g * 8 + 8):
                    total = members[j, k, 0].astype(jnp.float32) * wide[0]
                    for v in range(1, n_mem):
                        total = total + members[j, k, v].astype(jnp.float32) * wide[v]
                    total = ens_coef * total
                    for l in range(2):
                        turned[l, j, k * 8:(k + 1) * 8, :] = total[l * rows:(l + 1) * rows]

            for l in range(2):
                @pl.loop(0, tiles // 2)
                def _(jj):
                    for r in range(rows):
                        pair_of = [
                            turned[l, jj * 2 + half, pl.ds(g * 64 + r, 8, stride=8), :]
                            for half in range(2)
                        ]
                        for half in range(2):
                            field[l, rows + r, g, jj * 2 + half] = pair_of[half]
                        send_back[it, l, g, r, jj] = jnp.concatenate(pair_of, 0).astype(
                            jnp.bfloat16
                        )

                row_start(*back_args(it, l, g))

        row_wait(*static_args(it))
        for l in range(2):
            diffuse_static(it, l)

        def arrive_and_diffuse(l, g):
            row_wait(*back_args(it, l, g))

            @pl.loop(0, rows)
            def _(r):
                for jj in range(tiles // 2):
                    for side in range(2):
                        value = back_halo[it, side, l, g, r, jj].astype(jnp.float32)
                        for half in range(2):
                            field[l, side * 2 * rows + r, g, jj * 2 + half] = value[
                                half * 8:(half + 1) * 8
                            ]

            diffuse(it, l, g)

        @pl.loop(0, 2)
        def _(l):
            arrive_and_diffuse(l, 0)

        for l in range(2):
            if it == 0 and l == 1:
                for copy in obs_across():
                    copy.start()
                for i, ref in enumerate((obs_all, cut_all)):
                    for copy in obs_along(i, ref, me_m, 0):
                        copy.start()
            arrive_and_diffuse(l, 1)

            @pl.loop(0, tiles // 2)
            def _(jj):
                totals = []
                for half in range(2):
                    j = jj * 2 + half
                    total = [None] * n_mem
                    for k in range(16):
                        s = spread[l, j, pl.ds(k, 8, stride=16), :]
                        for v in range(n_mem):
                            m = members[j, k, v, l * rows:(l + 1) * rows, :].astype(jnp.float32)
                            total[v] = m * s if k == 0 else total[v] + m * s
                    totals.append(total)
                for v in range(n_mem):
                    partial[it, l, v, jj] = jnp.concatenate(
                        [totals[0][v], totals[1][v]], 0
                    ).astype(jnp.bfloat16)

            for d in same_rows:
                part_copy(it, l, d).start()
            arrived[it, l, me_m] = partial[it, l, me_m]

        curv = jnp.zeros((8, LANES), jnp.float32)
        for l in range(2):
            bytes_wait(arrived.at[it, l], n_mem - 1, part_recv.at[it, l])
            total = arrived[it, l, 0].astype(jnp.float32)
            for v in range(1, n_mem):
                total = total + arrived[it, l, v].astype(jnp.float32)
            for j in range(tiles):
                part = total[j // 2, (j % 2) * 8:(j % 2) * 8 + 8]
                img = ens_coef * part + stat_part[l, j]
                image[l, j] = img
                cut = cutoff(l, j)
                misfit = 0.0 - lane_tile(observed, l, j)
                if it > 0:
                    misfit = increment[l, j] + misfit
                weight = cut / jnp.maximum(jnp.abs(misfit), jnp.where(cut == 0.0, 1.0, cut))
                curv = curv + weight * img * img

        if it == 0:
            for copy in obs_across():
                copy.wait_recv()
        first[it, my_plane] = jnp.concatenate(
            [
                jnp.sum(norm_acc[...], axis=0, keepdims=True),
                jnp.sum(curv, axis=0, keepdims=True),
            ],
            1,
        )
        for d in planes:
            first_copy(it, d).start()
        if it == 0:
            for j in range(tiles):
                image_all[me_m, j] = jnp.concatenate([image[0, j], image[1, j]], 0).astype(
                    jnp.bfloat16
                )
            for d in same_rows:
                gather_copy(image_all, image_send, image_recv, d).start()
            for i, ref in enumerate((obs_all, cut_all)):
                for copy in obs_along(i, ref, partner, 1):
                    copy.start()
        bytes_wait(first.at[it], n_first - 1, small_recv.at[it, 0])
        second[it, z] = jnp.sum(first[it], axis=0)
        for d in along_z:
            second_copy(it, d).start()
        if it == 0:
            for i, ref in enumerate((obs_all, cut_all)):
                for k in range(2):
                    bytes_wait(ref, 3, obs_recv.at[2 + 2 * i + k])
            bytes_wait(image_all, n_mem - 1, image_recv)
        else:
            for n, out in enumerate((control_o, grad_nat)):
                @pl.loop(0, tiles)
                def _(j):
                    for l in range(2):
                        for r in range(rows):
                            for g in range(2):
                                value = grad[n, l, SWEEPS + r, g, j]
                                if n == 0:
                                    value = 0.0 - step_ref[...] * value
                                spread[l, j, r * 16 + g * 8:r * 16 + g * 8 + 8, :] = value

                for j in range(tiles):
                    for l in range(2):
                        for k in range(16):
                            out[k, l, :, j * LANES:(j + 1) * LANES] = spread[
                                l, j, pl.ds(k, 8, stride=16), :
                            ]
        bytes_wait(second.at[it], n_second - 1, small_recv.at[it, 1])
        sums = jnp.sum(second[it], axis=0)
        norm = jnp.sum(sums[:, :LANES], axis=1, keepdims=True)
        curvature = jnp.sum(sums[:, LANES:], axis=1, keepdims=True)
        step = jnp.broadcast_to(norm / (norm + curvature), (8, LANES))
        if it == 0:
            step_ref[...] = step
            next_sent(1, step)
            static_source(1)
            increment[...] = 0.0 - step * image[...]
        else:
            @pl.loop(0, control_o.shape[0])
            def _(k):
                for l in range(2):
                    for j in range(tiles):
                        lanes = slice(j * LANES, (j + 1) * LANES)
                        control_o[k, l, :, lanes] = (
                            control_o[k, l, :, lanes] - step * grad_nat[k, l, :, lanes]
                        )
            for l in range(2):
                for j in range(tiles):
                    lanes = slice(j * LANES, (j + 1) * LANES)
                    own = slice(rows, 2 * rows)
                    static_o[l, :, lanes] = (
                        0.0 - step_ref[...] * stat_grad[0, l, j, own] - step * stat_grad[1, l, j, own]
                    )
                    increment_o[l, :, lanes] = increment[l, j] - step * image[l, j]

    row_wait_send(*index_args)
    bytes_wait(sent_all.at[0], n_mem - 1, sent_send)
    bytes_wait(image_all, n_mem - 1, image_send)
    for copy in obs_across():
        copy.wait_send()
    for i, ref in enumerate((obs_all, cut_all)):
        for k in range(2):
            bytes_wait(ref, 3, obs_send.at[2 + 2 * i + k])
    for it in range(ITERS):
        row_wait_send(*static_args(it))
        for l in range(2):
            for g in range(2):
                row_wait_send(*back_args(it, l, g))
            bytes_wait(arrived.at[it, l], n_mem - 1, part_send.at[it, l])
        bytes_wait(first.at[it], n_first - 1, small_send.at[it, 0])
        bytes_wait(second.at[it], n_second - 1, small_send.at[it, 1])


def local(n_mem, n_row, members, static_scale, observed, huber_class, scale_index):
    k, v, _, rows, cells = members.shape
    ens_coef = math.sqrt(0.7 / (k * n_mem - 1))
    f32, bf16 = jnp.float32, jnp.bfloat16
    tiles = cells // LANES
    V = pltpu.VMEM
    scratch = [
        V((tiles, k, v, 16, LANES), bf16),
        V((2, rows, cells), f32),
        V((2, rows, cells), f32),
        V((2, rows, cells), jnp.int32),
        V((2, rows, cells), jnp.int32),
        V((ITERS, n_mem, tiles, 16, LANES), bf16),
        V((ITERS, tiles, 16, LANES), bf16),
        V((ITERS, 2, tiles, 16, LANES), bf16),
        V((tiles, 16, LANES), bf16),
        V((2, tiles, 16, LANES), bf16),
        V((n_mem, tiles, 16, LANES), f32),
        V((n_mem, tiles, 16, LANES), bf16),
        V((n_mem, tiles, 16, LANES), bf16),
        V((2, 3 * rows, tiles, 8, LANES), f32),
        V((2, tiles, 3 * rows, LANES), f32),
        V((2, tiles, k * rows, LANES), f32),
        V((2, 3 * rows, 2, tiles, 8, LANES), f32),
        V((ITERS, 2, 2, rows, tiles // 2, 16, LANES), bf16),
        V((ITERS, 2, 2, 2, rows, tiles // 2, 16, LANES), bf16),
        V((ITERS, 2, 2 * rows, 2, tiles, 8, LANES), f32),
        V((2, tiles, k * rows, LANES), f32),
        V((ITERS, 2, n_mem, tiles // 2, 16, LANES), bf16),
        V((ITERS, 2, n_mem, tiles // 2, 16, LANES), bf16),
        V((ITERS, 2, tiles, 3 * rows, LANES), f32),
        V((2, tiles, rows, LANES), f32),
        V((2, tiles, rows, LANES), f32),
        V((2, tiles, rows, LANES), f32),
        V((2, tiles, rows, LANES), f32),
        V((8, LANES), f32),
        V((8, LANES), f32),
        V((ITERS, 32, 1, 2 * LANES), f32),
        V((ITERS, 8, 1, 2 * LANES), f32),
        pltpu.SemaphoreType.DMA((4 + tiles,)),
        pltpu.SemaphoreType.DMA,
        pltpu.SemaphoreType.DMA,
        pltpu.SemaphoreType.DMA((ITERS * 5 + 1, 2)),
        pltpu.SemaphoreType.DMA((ITERS * 5 + 1, 2)),
        pltpu.SemaphoreType.DMA((ITERS, 2)),
        pltpu.SemaphoreType.DMA((ITERS, 2)),
        V((k, 2, rows, cells), f32),
        pltpu.SemaphoreType.DMA((ITERS, 2)),
        pltpu.SemaphoreType.DMA((ITERS, 2)),
        pltpu.SemaphoreType.DMA((6,)),
        pltpu.SemaphoreType.DMA((6,)),
        pltpu.SemaphoreType.DMA,
        pltpu.SemaphoreType.DMA,
    ]
    hbm = pl.BlockSpec(memory_space=pltpu.HBM)
    vmem = pl.BlockSpec(memory_space=pltpu.VMEM)
    wide = (k, 2, rows, cells)
    thin = (2, rows, cells)
    state = pl.pallas_call(
        functools.partial(kernel, n_mem, n_row, ens_coef),
        out_shape=[pltpu.VMEM(wide, f32), pltpu.VMEM(thin, f32), pltpu.VMEM(thin, f32)],
        in_specs=[hbm] * 5,
        out_specs=[vmem] * 3,
        scratch_shapes=scratch,
        compiler_params=pltpu.CompilerParams(
            collective_id=0, has_side_effects=True, vmem_limit_bytes=60 * 1024 * 1024
        ),
    )(
        members.reshape(k, v, 2 * rows, cells),
        static_scale[0],
        observed[0],
        huber_class[0],
        scale_index,
    )
    control, static_control, increment = state
    return control, static_control[None], increment[None]


def solution(mesh):
    sizes = dict(mesh.shape)
    placed = (
        P("mem", None, None, "row", None),
        P("mem", None, "row", None),
        P("mem", None, "row", None),
        P("mem", None, "row", None),
        P(None, "row", None),
    )
    return jax.shard_map(
        functools.partial(local, sizes["mem"], sizes["row"]),
        mesh=mesh,
        in_specs=placed,
        out_specs=(P("mem", None, "row", None),) * 3,
        check_vma=False,
    )
```

```python
import functools
import math

import jax
import jax.numpy as jnp
from jax import lax
from jax.experimental import pallas as pl
from jax.experimental.pallas import tpu as pltpu
from jax.sharding import PartitionSpec as P

SWEEPS = 4
ITERS = 2
KAPPAS = (0.06, 0.11, 0.17, 0.23)
LANES = 128
STAT = math.sqrt(0.3)
MESH = pl.DeviceIdType.MESH


def sideways(w):
    lane = lax.broadcasted_iota(jnp.int32, w.shape[1:], 1)[None]
    edge = jnp.zeros_like(w[:1])
    right = pltpu.roll(w, 1, 2)
    left = pltpu.roll(w, LANES - 1, 2)
    from_left = jnp.where(lane == 0, jnp.concatenate([edge, right[:-1]], 0), right)
    from_right = jnp.where(lane == LANES - 1, jnp.concatenate([left[1:], edge], 0), left)
    return from_left + from_right


def kernel(
    n_mem, n_row, ens_coef,
    members_h, scale_h, observed_h, huber_h, index_h,
    control_o, static_o, increment_o,
    members, scale, observed, huber, index,
    sent_all, send_static, static_halo, send_index, index_halo,
    seen_all, image_all,
    kwide, knat, turned, field, send_back, back_halo,
    grad, spread, partial, arrived,
    stat_grad, stat_back, stat_part, image, increment, norm_acc, step_ref, first, second,
    load_sem, sent_send, sent_recv, halo_send, halo_recv, part_send, part_recv,
    grad_nat, small_send, small_recv, obs_send, obs_recv, image_send, image_recv,
):
    me_m = lax.axis_index("mem")
    me_r = lax.axis_index("row")
    rows = 8
    tiles = 4
    has_low = me_r > 0
    has_high = me_r < n_row - 1

    def to(m, r):
        return {"mem": m, "row": r}

    loads = [
        pltpu.make_async_copy(observed_h, observed, load_sem.at[0]),
        pltpu.make_async_copy(huber_h, huber, load_sem.at[1]),
        pltpu.make_async_copy(index_h, index, load_sem.at[2]),
        pltpu.make_async_copy(scale_h, scale, load_sem.at[3]),
    ] + [
        pltpu.make_async_copy(
            members_h.at[:, :, :, pl.ds(j * LANES, LANES)], members.at[j], load_sem.at[4 + j]
        )
        for j in range(tiles)
    ]
    for load in loads:
        load.start()

    z_hi, y = me_m // 4, lax.rem(me_m, 4)
    x, z_lo, core = me_r // 8, lax.rem(me_r // 2, 4), lax.rem(me_r, 2)
    z = z_hi * 4 + z_lo

    def device_at(dx, dy, dz, dc):
        zz = lax.rem(z + dz, 8)
        m = (zz // 4) * 4 + lax.rem(y + dy, 4)
        r = lax.rem(x + dx, 4) * 8 + lax.rem(zz, 4) * 2 + lax.rem(core + dc, 2)
        return m, r

    def hops(d):
        return -(min(d[0], 4 - d[0]) + min(d[1], 4 - d[1]) + min(d[2], 8 - d[2]))

    planes = [(dx, dy, 0, dc) for dx in range(4) for dy in range(4) for dc in range(2)]
    planes = sorted(planes[1:], key=hops)
    along_z = sorted([(0, 0, dz, 0) for dz in range(1, 8)], key=hops)
    same_rows = sorted([(0, dy, dz, 0) for dz in (0, 4) for dy in range(4)][1:], key=hops)
    my_plane = (x * 4 + y) * 2 + core
    n_first, n_second = 32, 8

    greeted = sorted(set(planes + along_z + same_rows), key=hops)
    barrier = pltpu.get_barrier_semaphore()
    for d in greeted:
        pl.semaphore_signal(barrier, inc=1, device_id=to(*device_at(*d)), device_id_type=MESH)
    far = jnp.where(core == 0, me_r - 1, me_r + 1)
    has_far = jnp.logical_and(far >= 0, far < n_row)

    @pl.when(has_far)
    def _():
        pl.semaphore_signal(barrier, inc=1, device_id=to(me_m, far), device_id_type=MESH)

    def lane_tile(ref, l, j):
        return ref[l, :, j * LANES:(j + 1) * LANES]

    def cutoff(l, j):
        h = lane_tile(huber, l, j)
        return jnp.where(h == 1, 0.5, jnp.where(h == 2, 1.0, jnp.where(h == 3, 2.0, 0.0))).astype(
            jnp.float32
        )

    for load in loads[:4]:
        load.wait()
    for j in range(tiles):
        send_index[j] = jnp.concatenate(
            [lane_tile(index, 0, j), lane_tile(index, 1, j)], 0
        ).astype(jnp.float32).astype(jnp.bfloat16)

    @pl.when(jnp.logical_not(has_low))
    def _():
        index_halo[0] = jnp.full(index_halo.shape[1:], -1.0, jnp.bfloat16)
        static_halo[:, 0] = jnp.zeros_like(static_halo[:, 0])
        for it in range(ITERS):
            for l in range(2):
                for g in range(2):
                    back_halo[it, 0, l, g] = jnp.zeros_like(back_halo[it, 0, l, g])

    @pl.when(jnp.logical_not(has_high))
    def _():
        index_halo[1] = jnp.full(index_halo.shape[1:], -1.0, jnp.bfloat16)
        static_halo[:, 1] = jnp.zeros_like(static_halo[:, 1])
        for it in range(ITERS):
            for l in range(2):
                for g in range(2):
                    back_halo[it, 1, l, g] = jnp.zeros_like(back_halo[it, 1, l, g])

    def static_source(it):
        for j in range(tiles):
            wide = sent_all[it, me_m, j].astype(jnp.float32)
            for l in range(2):
                stat_back[l, j] = STAT * lane_tile(scale, l, j) * wide[l * rows:(l + 1) * rows]
            send_static[it, j] = jnp.concatenate(
                [stat_back[0, j], stat_back[1, j]], 0
            ).astype(jnp.bfloat16)

    def first_sent():
        for j in range(tiles):
            cut = jnp.concatenate([cutoff(0, j), cutoff(1, j)], 0)
            seen = jnp.concatenate([lane_tile(observed, 0, j), lane_tile(observed, 1, j)], 0)
            seen_all[me_m, j] = seen.astype(jnp.bfloat16)
            seen_all[me_m, tiles + j] = cut.astype(jnp.bfloat16)
            sent_all[0, me_m, j] = jnp.minimum(jnp.maximum(0.0 - seen, -cut), cut).astype(
                jnp.bfloat16
            )

    def next_sent(it, step):
        both = jnp.concatenate([step, step], 0)

        @pl.loop(0, n_mem)
        def _(v):
            for j in range(tiles):
                cut = seen_all[v, tiles + j].astype(jnp.float32)
                seen = seen_all[v, j].astype(jnp.float32)
                misfit = 0.0 - both * image_all[v, j].astype(jnp.float32) - seen
                sent_all[it, v, j] = jnp.minimum(jnp.maximum(misfit, -cut), cut).astype(
                    jnp.bfloat16
                )

    def rowcopy(src, dst_at, slot, side):
        target = me_r + 1 if side == 0 else me_r - 1
        return pltpu.make_async_remote_copy(
            src_ref=src, dst_ref=dst_at(side), send_sem=halo_send.at[slot, side],
            recv_sem=halo_recv.at[slot, side], device_id=to(me_m, target), device_id_type=MESH,
        )

    def row_start(src, dst_at, slot):
        @pl.when(has_high)
        def _():
            rowcopy(src, dst_at, slot, 0).start()

        @pl.when(has_low)
        def _():
            rowcopy(src, dst_at, slot, 1).start()

    def row_wait(src, dst_at, slot):
        @pl.when(has_low)
        def _():
            rowcopy(src, dst_at, slot, 0).wait_recv()

        @pl.when(has_high)
        def _():
            rowcopy(src, dst_at, slot, 1).wait_recv()

    def row_wait_send(src, dst_at, slot):
        @pl.when(has_high)
        def _():
            rowcopy(src, dst_at, slot, 0).wait_send()

        @pl.when(has_low)
        def _():
            rowcopy(src, dst_at, slot, 1).wait_send()

    n_slot = 5
    index_args = (send_index, lambda side: index_halo.at[side], ITERS * n_slot)

    def static_args(it):
        return send_static.at[it], lambda side: static_halo.at[it, side], it * n_slot

    def back_args(it, l, g):
        slot = it * n_slot + 1 + g * 2 + l
        return send_back.at[it, l, g], lambda side: back_halo.at[it, side, l, g], slot

    def push(src, dst, send, recv, device):
        return pltpu.make_async_remote_copy(
            src_ref=src, dst_ref=dst, send_sem=send, recv_sem=recv,
            device_id=to(*device), device_id_type=MESH,
        )

    def gather_copy(ref, send, recv, d):
        return push(ref.at[me_m], ref.at[me_m], send, recv, device_at(*d))

    def part_copy(it, l, d):
        v, r = device_at(*d)
        return push(
            partial.at[it, l, v], arrived.at[it, l, me_m],
            part_send.at[it, l], part_recv.at[it, l], (v, r),
        )

    def first_copy(it, d):
        own = first.at[it, my_plane]
        return push(own, own, small_send.at[it, 0], small_recv.at[it, 0], device_at(*d))

    def second_copy(it, d):
        own = second.at[it, z]
        return push(own, own, small_send.at[it, 1], small_recv.at[it, 1], device_at(*d))

    across = (0, 0, 4, 0)
    partner = lax.rem(me_m + 4, 8)
    along_y = [(0, dy, 0, 0) for dy in (2, 1, 3)]

    def seen_across():
        own = seen_all.at[me_m]
        return push(own, own, obs_send.at[0], obs_recv.at[0], device_at(*across))

    def seen_along(slot, k):
        own = seen_all.at[slot]
        return [push(own, own, obs_send.at[k], obs_recv.at[k], device_at(*d)) for d in along_y]

    def bytes_wait(ref, count, sem):
        part = ref.at[pl.ds(0, count)]
        pltpu.make_async_copy(part, part, sem).wait()

    def diffuse(it, l, g):
        low_in = jnp.where(has_low, 1.0, 0.0).astype(jnp.float32)
        high_in = jnp.where(has_high, 1.0, 0.0).astype(jnp.float32)
        for sweep in range(SWEEPS):
            lo, hi = sweep, 3 * rows - sweep

            def get(row):
                u = field[l, row, g]
                return u, u * kwide[l, row]

            _, w_prev = get(lo)
            u_cur, w_cur = get(lo + 1)
            norm = jnp.zeros((8, LANES), jnp.float32)
            for row in range(lo + 1, hi - 1):
                u_next, w_next = get(row + 1)
                out = (w_prev + w_next) + sideways(w_cur) + (u_cur - 4.0 * w_cur)
                if sweep < SWEEPS - 1:
                    field[l, row, g] = out
                else:
                    if it > 0:
                        out = out - step_ref[...] * grad[0, l, row - SWEEPS, g]
                    if row < rows:
                        out = out * low_in
                    elif row >= 2 * rows:
                        out = out * high_in
                    else:
                        norm = norm + jnp.sum(out * out, axis=0)
                    grad[it, l, row - SWEEPS, g] = out
                w_prev, u_cur, w_cur = w_cur, u_next, w_next
        norm_acc[...] += norm
        for sweep in range(SWEEPS):
            lo, hi = SWEEPS + sweep, 3 * rows - SWEEPS - sweep

            def load(row):
                return grad[it, l, row - SWEEPS, g] if sweep == 0 else field[l, row, g]

            u_prev, u_cur = load(lo), load(lo + 1)
            for row in range(lo + 1, hi - 1):
                u_next = load(row + 1)
                out = u_cur + kwide[l, row] * ((u_prev + u_next) + sideways(u_cur) - 4.0 * u_cur)
                if sweep < SWEEPS - 1:
                    field[l, row, g] = out
                else:
                    out = out.astype(jnp.bfloat16).astype(jnp.float32)
                    for j in range(tiles):
                        spread[l, j, pl.ds((row - rows) * 16 + g * 8, 8), :] = out[j]
                u_prev, u_cur = u_cur, u_next

    def diffuse_static(it, l):
        halo = static_halo[it].astype(jnp.float32)
        here = slice(l * rows, (l + 1) * rows)
        u = jnp.concatenate([halo[0, :, here], stat_back[l], halo[1, :, here]], 1)
        k = knat[l]
        grow = me_r * rows - rows + lax.broadcasted_iota(jnp.int32, (3 * rows, LANES), 0)
        inside = jnp.logical_and(grow >= 0, grow < n_row * rows)[None]
        n = 3 * rows
        for sweep in range(SWEEPS):
            w = k * u
            u = (pltpu.roll(w, 1, 1) + pltpu.roll(w, n - 1, 1)) + sideways(w) + (u - 4.0 * w)
        if it > 0:
            u = u - step_ref[:1] * stat_grad[0, l]
        u = jnp.where(inside, u, 0.0)
        stat_grad[it, l] = u
        own = u[:, rows:2 * rows]
        norm_acc[...] += jnp.sum(own * own, axis=0)
        for sweep in range(SWEEPS):
            u = u + k * (
                (pltpu.roll(u, 1, 1) + pltpu.roll(u, n - 1, 1)) + sideways(u) - 4.0 * u
            )
        for j in range(tiles):
            stat_part[l, j] = STAT * lane_tile(scale, l, j) * u[j, rows:2 * rows]

    first_sent()
    static_source(0)

    @pl.when(has_far)
    def _():
        pl.semaphore_wait(barrier, len(greeted) + 1)

    @pl.when(jnp.logical_not(has_far))
    def _():
        pl.semaphore_wait(barrier, len(greeted))

    for it in range(ITERS):
        if it == 0:
            for d in same_rows:
                gather_copy(sent_all.at[0], sent_send, sent_recv, d).start()
            row_start(*index_args)
            seen_across().start()
        row_start(*static_args(it))
        norm_acc[...] = jnp.zeros_like(norm_acc)
        if it == 0:
            row_wait(*index_args)
            for j in range(tiles):
                for l in range(2):
                    here = slice(l * rows, (l + 1) * rows)
                    both = index_halo[:, j].astype(jnp.float32)
                    ids = jnp.concatenate(
                        [both[0, here], lane_tile(index, l, j).astype(jnp.float32), both[1, here]],
                        0,
                    )
                    k = jnp.zeros_like(ids)
                    for i, value in enumerate(KAPPAS):
                        k = jnp.where(ids == i, value, k)
                    knat[l, j] = k
                    for row in range(3 * rows):
                        kwide[l, row, j] = jnp.broadcast_to(k[row:row + 1], (8, LANES))
            for load in loads[4:]:
                load.wait()
            bytes_wait(sent_all.at[0], n_mem - 1, sent_recv)

        for g in range(2):
            @pl.loop(0, tiles)
            def _(j):
                wide = [sent_all[it, v, j].astype(jnp.float32) for v in range(n_mem)]
                for k in range(g * 8, g * 8 + 8):
                    total = members[j, k, 0].astype(jnp.float32) * wide[0]
                    for v in range(1, n_mem):
                        total = total + members[j, k, v].astype(jnp.float32) * wide[v]
                    total = ens_coef * total
                    for l in range(2):
                        turned[l, j, k * 8:(k + 1) * 8, :] = total[l * rows:(l + 1) * rows]

            for l in range(2):
                @pl.loop(0, tiles // 2)
                def _(jj):
                    for r in range(rows):
                        pair_of = [
                            turned[l, jj * 2 + half, pl.ds(g * 64 + r, 8, stride=8), :]
                            for half in range(2)
                        ]
                        for half in range(2):
                            field[l, rows + r, g, jj * 2 + half] = pair_of[half]
                        send_back[it, l, g, r, jj] = jnp.concatenate(pair_of, 0).astype(
                            jnp.bfloat16
                        )

                row_start(*back_args(it, l, g))

        if it == 0:
            for copy in seen_along(me_m, 1):
                copy.start()
            seen_across().wait_recv()
            for copy in seen_along(partner, 2):
                copy.start()
        row_wait(*static_args(it))
        for l in range(2):
            diffuse_static(it, l)

        def arrive_and_diffuse(l, g):
            row_wait(*back_args(it, l, g))

            @pl.loop(0, rows)
            def _(r):
                for jj in range(tiles // 2):
                    for side in range(2):
                        value = back_halo[it, side, l, g, r, jj].astype(jnp.float32)
                        for half in range(2):
                            field[l, side * 2 * rows + r, g, jj * 2 + half] = value[
                                half * 8:(half + 1) * 8
                            ]

            diffuse(it, l, g)

        @pl.loop(0, 2)
        def _(l):
            arrive_and_diffuse(l, 0)

        for l in range(2):
            arrive_and_diffuse(l, 1)

            @pl.loop(0, tiles // 2)
            def _(jj):
                totals = []
                for half in range(2):
                    j = jj * 2 + half
                    total = [None] * n_mem
                    for k in range(16):
                        s = spread[l, j, pl.ds(k, 8, stride=16), :]
                        for v in range(n_mem):
                            m = members[j, k, v, l * rows:(l + 1) * rows, :].astype(jnp.float32)
                            total[v] = m * s if k == 0 else total[v] + m * s
                    totals.append(total)
                for v in range(n_mem):
                    partial[it, l, v, jj] = jnp.concatenate(
                        [totals[0][v], totals[1][v]], 0
                    ).astype(jnp.bfloat16)

            for d in same_rows:
                part_copy(it, l, d).start()
            arrived[it, l, me_m] = partial[it, l, me_m]

        curv = jnp.zeros((8, LANES), jnp.float32)
        for l in range(2):
            bytes_wait(arrived.at[it, l], n_mem - 1, part_recv.at[it, l])
            total = arrived[it, l, 0].astype(jnp.float32)
            for v in range(1, n_mem):
                total = total + arrived[it, l, v].astype(jnp.float32)
            for j in range(tiles):
                part = total[j // 2, (j % 2) * 8:(j % 2) * 8 + 8]
                img = ens_coef * part + stat_part[l, j]
                image[l, j] = img
                cut = cutoff(l, j)
                misfit = 0.0 - lane_tile(observed, l, j)
                if it > 0:
                    misfit = increment[l, j] + misfit
                weight = cut / jnp.maximum(jnp.abs(misfit), jnp.where(cut == 0.0, 1.0, cut))
                curv = curv + weight * img * img

        first[it, my_plane] = jnp.concatenate(
            [
                jnp.sum(norm_acc[...], axis=0, keepdims=True),
                jnp.sum(curv, axis=0, keepdims=True),
            ],
            1,
        )
        for d in planes:
            first_copy(it, d).start()
        if it == 0:
            for j in range(tiles):
                image_all[me_m, j] = jnp.concatenate([image[0, j], image[1, j]], 0).astype(
                    jnp.bfloat16
                )
            for d in same_rows:
                gather_copy(image_all, image_send, image_recv, d).start()
        bytes_wait(first.at[it], n_first - 1, small_recv.at[it, 0])
        second[it, z] = jnp.sum(first[it], axis=0)
        for d in along_z:
            second_copy(it, d).start()
        if it == 0:
            for k in (1, 2):
                bytes_wait(seen_all, 3, obs_recv.at[k])
            bytes_wait(image_all, n_mem - 1, image_recv)
        else:
            for n, out in enumerate((control_o, grad_nat)):
                @pl.loop(0, tiles)
                def _(j):
                    for l in range(2):
                        for r in range(rows):
                            for g in range(2):
                                value = grad[n, l, SWEEPS + r, g, j]
                                if n == 0:
                                    value = 0.0 - step_ref[...] * value
                                spread[l, j, r * 16 + g * 8:r * 16 + g * 8 + 8, :] = value

                for j in range(tiles):
                    for l in range(2):
                        for k in range(16):
                            out[k, l, :, j * LANES:(j + 1) * LANES] = spread[
                                l, j, pl.ds(k, 8, stride=16), :
                            ]
        bytes_wait(second.at[it], n_second - 1, small_recv.at[it, 1])
        sums = jnp.sum(second[it], axis=0)
        norm = jnp.sum(sums[:, :LANES], axis=1, keepdims=True)
        curvature = jnp.sum(sums[:, LANES:], axis=1, keepdims=True)
        step = jnp.broadcast_to(norm / (norm + curvature), (8, LANES))
        if it == 0:
            step_ref[...] = step
            next_sent(1, step)
            static_source(1)
            increment[...] = 0.0 - step * image[...]
        else:
            @pl.loop(0, control_o.shape[0])
            def _(k):
                for l in range(2):
                    for j in range(tiles):
                        lanes = slice(j * LANES, (j + 1) * LANES)
                        control_o[k, l, :, lanes] = (
                            control_o[k, l, :, lanes] - step * grad_nat[k, l, :, lanes]
                        )
            for l in range(2):
                for j in range(tiles):
                    lanes = slice(j * LANES, (j + 1) * LANES)
                    own = slice(rows, 2 * rows)
                    static_o[l, :, lanes] = (
                        0.0 - step_ref[...] * stat_grad[0, l, j, own] - step * stat_grad[1, l, j, own]
                    )
                    increment_o[l, :, lanes] = increment[l, j] - step * image[l, j]

    row_wait_send(*index_args)
    bytes_wait(sent_all.at[0], n_mem - 1, sent_send)
    bytes_wait(image_all, n_mem - 1, image_send)
    seen_across().wait_send()
    for k in (1, 2):
        bytes_wait(seen_all, 3, obs_send.at[k])
    for it in range(ITERS):
        row_wait_send(*static_args(it))
        for l in range(2):
            for g in range(2):
                row_wait_send(*back_args(it, l, g))
            bytes_wait(arrived.at[it, l], n_mem - 1, part_send.at[it, l])
        bytes_wait(first.at[it], n_first - 1, small_send.at[it, 0])
        bytes_wait(second.at[it], n_second - 1, small_send.at[it, 1])


def local(n_mem, n_row, members, static_scale, observed, huber_class, scale_index):
    k, v, _, rows, cells = members.shape
    ens_coef = math.sqrt(0.7 / (k * n_mem - 1))
    f32, bf16 = jnp.float32, jnp.bfloat16
    tiles = cells // LANES
    V = pltpu.VMEM
    scratch = [
        V((tiles, k, v, 16, LANES), bf16),
        V((2, rows, cells), f32),
        V((2, rows, cells), f32),
        V((2, rows, cells), jnp.int32),
        V((2, rows, cells), jnp.int32),
        V((ITERS, n_mem, tiles, 16, LANES), bf16),
        V((ITERS, tiles, 16, LANES), bf16),
        V((ITERS, 2, tiles, 16, LANES), bf16),
        V((tiles, 16, LANES), bf16),
        V((2, tiles, 16, LANES), bf16),
        V((n_mem, 2 * tiles, 16, LANES), bf16),
        V((n_mem, tiles, 16, LANES), bf16),
        V((2, 3 * rows, tiles, 8, LANES), f32),
        V((2, tiles, 3 * rows, LANES), f32),
        V((2, tiles, k * rows, LANES), f32),
        V((2, 3 * rows, 2, tiles, 8, LANES), f32),
        V((ITERS, 2, 2, rows, tiles // 2, 16, LANES), bf16),
        V((ITERS, 2, 2, 2, rows, tiles // 2, 16, LANES), bf16),
        V((ITERS, 2, 2 * rows, 2, tiles, 8, LANES), f32),
        V((2, tiles, k * rows, LANES), f32),
        V((ITERS, 2, n_mem, tiles // 2, 16, LANES), bf16),
        V((ITERS, 2, n_mem, tiles // 2, 16, LANES), bf16),
        V((ITERS, 2, tiles, 3 * rows, LANES), f32),
        V((2, tiles, rows, LANES), f32),
        V((2, tiles, rows, LANES), f32),
        V((2, tiles, rows, LANES), f32),
        V((2, tiles, rows, LANES), f32),
        V((8, LANES), f32),
        V((8, LANES), f32),
        V((ITERS, 32, 1, 2 * LANES), f32),
        V((ITERS, 8, 1, 2 * LANES), f32),
        pltpu.SemaphoreType.DMA((4 + tiles,)),
        pltpu.SemaphoreType.DMA,
        pltpu.SemaphoreType.DMA,
        pltpu.SemaphoreType.DMA((ITERS * 5 + 1, 2)),
        pltpu.SemaphoreType.DMA((ITERS * 5 + 1, 2)),
        pltpu.SemaphoreType.DMA((ITERS, 2)),
        pltpu.SemaphoreType.DMA((ITERS, 2)),
        V((k, 2, rows, cells), f32),
        pltpu.SemaphoreType.DMA((ITERS, 2)),
        pltpu.SemaphoreType.DMA((ITERS, 2)),
        pltpu.SemaphoreType.DMA((3,)),
        pltpu.SemaphoreType.DMA((3,)),
        pltpu.SemaphoreType.DMA,
        pltpu.SemaphoreType.DMA,
    ]
    hbm = pl.BlockSpec(memory_space=pltpu.HBM)
    vmem = pl.BlockSpec(memory_space=pltpu.VMEM)
    wide = (k, 2, rows, cells)
    thin = (2, rows, cells)
    state = pl.pallas_call(
        functools.partial(kernel, n_mem, n_row, ens_coef),
        out_shape=[pltpu.VMEM(wide, f32), pltpu.VMEM(thin, f32), pltpu.VMEM(thin, f32)],
        in_specs=[hbm] * 5,
        out_specs=[vmem] * 3,
        scratch_shapes=scratch,
        compiler_params=pltpu.CompilerParams(
            collective_id=0, has_side_effects=True, vmem_limit_bytes=60 * 1024 * 1024
        ),
    )(
        members.reshape(k, v, 2 * rows, cells),
        static_scale[0],
        observed[0],
        huber_class[0],
        scale_index,
    )
    control, static_control, increment = state
    return control, static_control[None], increment[None]


def solution(mesh):
    sizes = dict(mesh.shape)
    placed = (
        P("mem", None, None, "row", None),
        P("mem", None, "row", None),
        P("mem", None, "row", None),
        P("mem", None, "row", None),
        P(None, "row", None),
    )
    return jax.shard_map(
        functools.partial(local, sizes["mem"], sizes["row"]),
        mesh=mesh,
        in_specs=placed,
        out_specs=(P("mem", None, "row", None),) * 3,
        check_vma=False,
    )
```

```python
import functools
import math

import jax
import jax.numpy as jnp
from jax import lax
from jax.experimental import pallas as pl
from jax.experimental.pallas import tpu as pltpu
from jax.sharding import PartitionSpec as P

SWEEPS = 4
ITERS = 2
KAPPAS = (0.06, 0.11, 0.17, 0.23)
LANES = 128
STAT = math.sqrt(0.3)
MESH = pl.DeviceIdType.MESH


def sideways(w):
    lane = lax.broadcasted_iota(jnp.int32, w.shape[1:], 1)[None]
    edge = jnp.zeros_like(w[:1])
    right = pltpu.roll(w, 1, 2)
    left = pltpu.roll(w, LANES - 1, 2)
    from_left = jnp.where(lane == 0, jnp.concatenate([edge, right[:-1]], 0), right)
    from_right = jnp.where(lane == LANES - 1, jnp.concatenate([left[1:], edge], 0), left)
    return from_left + from_right


def pick(tiles, index, source):
    out = None
    for t, tile in enumerate(tiles):
        moved = jnp.take_along_axis(tile, index, axis=1, mode="promise_in_bounds")
        out = moved if out is None else jnp.where(source == t, moved, out)
    return out


def interleave(tiles):
    lane = lax.broadcasted_iota(jnp.int32, tiles[0].shape, 1)
    return [pick(tiles, 4 * lax.rem(lane, 32) + j, lane // 32) for j in range(4)]


def in_order(tiles):
    lane = lax.broadcasted_iota(jnp.int32, tiles[0].shape, 1)
    return [pick(tiles, 32 * t + lane // 4, lax.rem(lane, 4)) for t in range(4)]


def sideways_interleaved(w):
    lane = lax.broadcasted_iota(jnp.int32, w.shape[1:], 1)
    before = jnp.where(lane == 0, 0.0, pltpu.roll(w[-1], 1, 1))[None]
    after = jnp.where(lane == LANES - 1, 0.0, pltpu.roll(w[0], LANES - 1, 1))[None]
    return jnp.concatenate([before, w[:-1]], 0) + jnp.concatenate([w[1:], after], 0)


def kernel(
    n_mem, n_row, ens_coef,
    members_h, scale_h, observed_h, huber_h, index_h,
    control_o, static_o, increment_o,
    members, scale, observed, huber, index,
    sent_all, send_static, static_halo, send_index, index_halo,
    seen_all, image_all,
    kwide, knat, turned, field, send_back, back_halo,
    grad, spread, partial, arrived,
    stat_grad, stat_back, stat_part, image, increment, norm_acc, step_ref, first, second,
    load_sem, sent_send, sent_recv, halo_send, halo_recv, part_send, part_recv,
    grad_nat, small_send, small_recv, obs_send, obs_recv, image_send, image_recv,
):
    me_m = lax.axis_index("mem")
    me_r = lax.axis_index("row")
    rows = 8
    tiles = 4
    has_low = me_r > 0
    has_high = me_r < n_row - 1

    def to(m, r):
        return {"mem": m, "row": r}

    loads = [
        pltpu.make_async_copy(observed_h, observed, load_sem.at[0]),
        pltpu.make_async_copy(huber_h, huber, load_sem.at[1]),
        pltpu.make_async_copy(index_h, index, load_sem.at[2]),
        pltpu.make_async_copy(scale_h, scale, load_sem.at[3]),
    ] + [
        pltpu.make_async_copy(
            members_h.at[:, :, :, pl.ds(j * LANES, LANES)], members.at[j], load_sem.at[4 + j]
        )
        for j in range(tiles)
    ]

    z_hi, y = me_m // 4, lax.rem(me_m, 4)
    x, z_lo, core = me_r // 8, lax.rem(me_r // 2, 4), lax.rem(me_r, 2)
    z = z_hi * 4 + z_lo

    def device_at(dx, dy, dz, dc):
        zz = lax.rem(z + dz, 8)
        m = (zz // 4) * 4 + lax.rem(y + dy, 4)
        r = lax.rem(x + dx, 4) * 8 + lax.rem(zz, 4) * 2 + lax.rem(core + dc, 2)
        return m, r

    def hops(d):
        return -(min(d[0], 4 - d[0]) + min(d[1], 4 - d[1]) + min(d[2], 8 - d[2]))

    planes = [(dx, dy, 0, dc) for dx in range(4) for dy in range(4) for dc in range(2)]
    planes = sorted(planes[1:], key=hops)
    along_z = sorted([(0, 0, dz, 0) for dz in range(1, 8)], key=hops)
    same_rows = sorted([(0, dy, dz, 0) for dz in (0, 4) for dy in range(4)][1:], key=hops)
    my_plane = (x * 4 + y) * 2 + core
    n_first, n_second = 32, 8

    greeted = sorted(set(planes + along_z + same_rows), key=hops)
    barrier = pltpu.get_barrier_semaphore()
    for d in greeted:
        pl.semaphore_signal(barrier, inc=1, device_id=to(*device_at(*d)), device_id_type=MESH)
    far = jnp.where(core == 0, me_r - 1, me_r + 1)
    has_far = jnp.logical_and(far >= 0, far < n_row)

    @pl.when(has_far)
    def _():
        pl.semaphore_signal(barrier, inc=1, device_id=to(me_m, far), device_id_type=MESH)

    for load in loads:
        load.start()

    def lane_tile(ref, l, j):
        return ref[l, :, j * LANES:(j + 1) * LANES]

    def cutoff(l, j):
        h = lane_tile(huber, l, j)
        return jnp.where(h == 1, 0.5, jnp.where(h == 2, 1.0, jnp.where(h == 3, 2.0, 0.0))).astype(
            jnp.float32
        )

    for load in loads[:4]:
        load.wait()
    for j in range(tiles):
        send_index[j] = jnp.concatenate(
            [lane_tile(index, 0, j), lane_tile(index, 1, j)], 0
        ).astype(jnp.float32).astype(jnp.bfloat16)

    @pl.when(jnp.logical_not(has_low))
    def _():
        index_halo[0] = jnp.full(index_halo.shape[1:], -1.0, jnp.bfloat16)
        static_halo[:, 0] = jnp.zeros_like(static_halo[:, 0])
        for it in range(ITERS):
            for l in range(2):
                for g in range(2):
                    back_halo[it, 0, l, g] = jnp.zeros_like(back_halo[it, 0, l, g])

    @pl.when(jnp.logical_not(has_high))
    def _():
        index_halo[1] = jnp.full(index_halo.shape[1:], -1.0, jnp.bfloat16)
        static_halo[:, 1] = jnp.zeros_like(static_halo[:, 1])
        for it in range(ITERS):
            for l in range(2):
                for g in range(2):
                    back_halo[it, 1, l, g] = jnp.zeros_like(back_halo[it, 1, l, g])

    def static_source(it):
        for j in range(tiles):
            wide = sent_all[it, me_m, j].astype(jnp.float32)
            for l in range(2):
                stat_back[l, j] = STAT * lane_tile(scale, l, j) * wide[l * rows:(l + 1) * rows]
            send_static[it, j] = jnp.concatenate(
                [stat_back[0, j], stat_back[1, j]], 0
            ).astype(jnp.bfloat16)

    def first_sent():
        for j in range(tiles):
            cut = jnp.concatenate([cutoff(0, j), cutoff(1, j)], 0)
            seen = jnp.concatenate([lane_tile(observed, 0, j), lane_tile(observed, 1, j)], 0)
            seen_all[me_m, j] = seen.astype(jnp.bfloat16)
            seen_all[me_m, tiles + j] = cut.astype(jnp.bfloat16)
            sent_all[0, me_m, j] = jnp.minimum(jnp.maximum(0.0 - seen, -cut), cut).astype(
                jnp.bfloat16
            )

    def next_sent(it, step):
        both = jnp.concatenate([step, step], 0)

        @pl.loop(0, n_mem)
        def _(v):
            for j in range(tiles):
                cut = seen_all[v, tiles + j].astype(jnp.float32)
                seen = seen_all[v, j].astype(jnp.float32)
                misfit = 0.0 - both * image_all[v, j].astype(jnp.float32) - seen
                sent_all[it, v, j] = jnp.minimum(jnp.maximum(misfit, -cut), cut).astype(
                    jnp.bfloat16
                )

    def rowcopy(src, dst_at, slot, side):
        target = me_r + 1 if side == 0 else me_r - 1
        return pltpu.make_async_remote_copy(
            src_ref=src, dst_ref=dst_at(side), send_sem=halo_send.at[slot, side],
            recv_sem=halo_recv.at[slot, side], device_id=to(me_m, target), device_id_type=MESH,
        )

    def row_start(src, dst_at, slot):
        @pl.when(has_high)
        def _():
            rowcopy(src, dst_at, slot, 0).start()

        @pl.when(has_low)
        def _():
            rowcopy(src, dst_at, slot, 1).start()

    def row_wait(src, dst_at, slot):
        @pl.when(has_low)
        def _():
            rowcopy(src, dst_at, slot, 0).wait_recv()

        @pl.when(has_high)
        def _():
            rowcopy(src, dst_at, slot, 1).wait_recv()

    def row_wait_send(src, dst_at, slot):
        @pl.when(has_high)
        def _():
            rowcopy(src, dst_at, slot, 0).wait_send()

        @pl.when(has_low)
        def _():
            rowcopy(src, dst_at, slot, 1).wait_send()

    n_slot = 5
    index_args = (send_index, lambda side: index_halo.at[side], ITERS * n_slot)

    def static_args(it):
        return send_static.at[it], lambda side: static_halo.at[it, side], it * n_slot

    def back_args(it, l, g):
        slot = it * n_slot + 1 + g * 2 + l
        return send_back.at[it, l, g], lambda side: back_halo.at[it, side, l, g], slot

    def push(src, dst, send, recv, device):
        return pltpu.make_async_remote_copy(
            src_ref=src, dst_ref=dst, send_sem=send, recv_sem=recv,
            device_id=to(*device), device_id_type=MESH,
        )

    def gather_copy(ref, send, recv, d):
        return push(ref.at[me_m], ref.at[me_m], send, recv, device_at(*d))

    def part_copy(it, l, d):
        v, r = device_at(*d)
        return push(
            partial.at[it, l, v], arrived.at[it, l, me_m],
            part_send.at[it, l], part_recv.at[it, l], (v, r),
        )

    def first_copy(it, d):
        own = first.at[it, my_plane]
        return push(own, own, small_send.at[it, 0], small_recv.at[it, 0], device_at(*d))

    def second_copy(it, d):
        own = second.at[it, z]
        return push(own, own, small_send.at[it, 1], small_recv.at[it, 1], device_at(*d))

    across = (0, 0, 4, 0)
    partner = lax.rem(me_m + 4, 8)
    along_y = [(0, dy, 0, 0) for dy in (2, 1, 3)]

    def seen_across():
        own = seen_all.at[me_m]
        return push(own, own, obs_send.at[0], obs_recv.at[0], device_at(*across))

    def seen_along(slot, k):
        own = seen_all.at[slot]
        return [push(own, own, obs_send.at[k], obs_recv.at[k], device_at(*d)) for d in along_y]

    def bytes_wait(ref, count, sem):
        part = ref.at[pl.ds(0, count)]
        pltpu.make_async_copy(part, part, sem).wait()

    def diffuse(it, l, g):
        low_in = jnp.where(has_low, 1.0, 0.0).astype(jnp.float32)
        high_in = jnp.where(has_high, 1.0, 0.0).astype(jnp.float32)
        for sweep in range(SWEEPS):
            lo, hi = sweep, 3 * rows - sweep

            def get(row):
                u = field[l, row, g]
                return u, u * kwide[l, row]

            _, w_prev = get(lo)
            u_cur, w_cur = get(lo + 1)
            norm = jnp.zeros((8, LANES), jnp.float32)
            for row in range(lo + 1, hi - 1):
                u_next, w_next = get(row + 1)
                out = (w_prev + w_next) + sideways_interleaved(w_cur) + (u_cur - 4.0 * w_cur)
                if sweep < SWEEPS - 1:
                    field[l, row, g] = out
                else:
                    if it > 0:
                        out = out - step_ref[...] * grad[0, l, row - SWEEPS, g]
                    if row < rows:
                        out = out * low_in
                    elif row >= 2 * rows:
                        out = out * high_in
                    else:
                        norm = norm + jnp.sum(out * out, axis=0)
                    grad[it, l, row - SWEEPS, g] = out
                w_prev, u_cur, w_cur = w_cur, u_next, w_next
        norm_acc[...] += norm
        for sweep in range(SWEEPS):
            lo, hi = SWEEPS + sweep, 3 * rows - SWEEPS - sweep

            def load(row):
                return grad[it, l, row - SWEEPS, g] if sweep == 0 else field[l, row, g]

            u_prev, u_cur = load(lo), load(lo + 1)
            for row in range(lo + 1, hi - 1):
                u_next = load(row + 1)
                out = u_cur + kwide[l, row] * ((u_prev + u_next) + sideways_interleaved(u_cur) - 4.0 * u_cur)
                if sweep < SWEEPS - 1:
                    field[l, row, g] = out
                else:
                    out = out.astype(jnp.bfloat16).astype(jnp.float32)
                    for j, tile in enumerate(in_order([out[j] for j in range(tiles)])):
                        spread[l, j, pl.ds((row - rows) * 16 + g * 8, 8), :] = tile
                u_prev, u_cur = u_cur, u_next

    def diffuse_static(it, l):
        halo = static_halo[it].astype(jnp.float32)
        here = slice(l * rows, (l + 1) * rows)
        u = jnp.concatenate([halo[0, :, here], stat_back[l], halo[1, :, here]], 1)
        k = knat[l]
        grow = me_r * rows - rows + lax.broadcasted_iota(jnp.int32, (3 * rows, LANES), 0)
        inside = jnp.logical_and(grow >= 0, grow < n_row * rows)[None]
        n = 3 * rows
        for sweep in range(SWEEPS):
            w = k * u
            u = (pltpu.roll(w, 1, 1) + pltpu.roll(w, n - 1, 1)) + sideways(w) + (u - 4.0 * w)
        if it > 0:
            u = u - step_ref[:1] * stat_grad[0, l]
        u = jnp.where(inside, u, 0.0)
        stat_grad[it, l] = u
        own = u[:, rows:2 * rows]
        norm_acc[...] += jnp.sum(own * own, axis=0)
        for sweep in range(SWEEPS):
            u = u + k * (
                (pltpu.roll(u, 1, 1) + pltpu.roll(u, n - 1, 1)) + sideways(u) - 4.0 * u
            )
        for j in range(tiles):
            stat_part[l, j] = STAT * lane_tile(scale, l, j) * u[j, rows:2 * rows]

    first_sent()
    static_source(0)

    @pl.when(has_far)
    def _():
        pl.semaphore_wait(barrier, len(greeted) + 1)

    @pl.when(jnp.logical_not(has_far))
    def _():
        pl.semaphore_wait(barrier, len(greeted))

    for it in range(ITERS):
        if it == 0:
            for d in same_rows:
                gather_copy(sent_all.at[0], sent_send, sent_recv, d).start()
            row_start(*index_args)
            seen_across().start()
        row_start(*static_args(it))
        norm_acc[...] = jnp.zeros_like(norm_acc)
        if it == 0:
            row_wait(*index_args)
            for j in range(tiles):
                for l in range(2):
                    here = slice(l * rows, (l + 1) * rows)
                    both = index_halo[:, j].astype(jnp.float32)
                    ids = jnp.concatenate(
                        [both[0, here], lane_tile(index, l, j).astype(jnp.float32), both[1, here]],
                        0,
                    )
                    k = jnp.zeros_like(ids)
                    for i, value in enumerate(KAPPAS):
                        k = jnp.where(ids == i, value, k)
                    knat[l, j] = k
            for l in range(2):
                for third in range(3):
                    here = slice(third * rows, (third + 1) * rows)
                    for j, tile in enumerate(interleave([knat[l, j, here] for j in range(tiles)])):
                        for r in range(rows):
                            kwide[l, third * rows + r, j] = jnp.broadcast_to(
                                tile[r:r + 1], (8, LANES)
                            )
            for load in loads[4:]:
                load.wait()
            bytes_wait(sent_all.at[0], n_mem - 1, sent_recv)

        for g in range(2):
            @pl.loop(0, tiles)
            def _(j):
                wide = [sent_all[it, v, j].astype(jnp.float32) for v in range(n_mem)]
                for k in range(g * 8, g * 8 + 8):
                    total = members[j, k, 0].astype(jnp.float32) * wide[0]
                    for v in range(1, n_mem):
                        total = total + members[j, k, v].astype(jnp.float32) * wide[v]
                    total = ens_coef * total
                    for l in range(2):
                        turned[l, j, k * 8:(k + 1) * 8, :] = total[l * rows:(l + 1) * rows]

            for l in range(2):
                for r in range(rows):
                    mixed = interleave(
                        [turned[l, j, pl.ds(g * 64 + r, 8, stride=8), :] for j in range(tiles)]
                    )
                    for j in range(tiles):
                        field[l, rows + r, g, j] = mixed[j]
                    for jj in range(tiles // 2):
                        send_back[it, l, g, r, jj] = jnp.concatenate(
                            mixed[2 * jj:2 * jj + 2], 0
                        ).astype(jnp.bfloat16)

                row_start(*back_args(it, l, g))

        if it == 0:
            for copy in seen_along(me_m, 1):
                copy.start()
            seen_across().wait_recv()
            for copy in seen_along(partner, 2):
                copy.start()

        def arrive_and_diffuse(l, g):
            row_wait(*back_args(it, l, g))

            @pl.loop(0, rows)
            def _(r):
                for jj in range(tiles // 2):
                    for side in range(2):
                        value = back_halo[it, side, l, g, r, jj].astype(jnp.float32)
                        for half in range(2):
                            field[l, side * 2 * rows + r, g, jj * 2 + half] = value[
                                half * 8:(half + 1) * 8
                            ]

            diffuse(it, l, g)

        @pl.loop(0, 2)
        def _(l):
            arrive_and_diffuse(l, 0)

        for l in range(2):
            arrive_and_diffuse(l, 1)

            @pl.loop(0, tiles // 2)
            def _(jj):
                totals = []
                for half in range(2):
                    j = jj * 2 + half
                    total = [None] * n_mem
                    for k in range(16):
                        s = spread[l, j, pl.ds(k, 8, stride=16), :]
                        for v in range(n_mem):
                            m = members[j, k, v, l * rows:(l + 1) * rows, :].astype(jnp.float32)
                            total[v] = m * s if k == 0 else total[v] + m * s
                    totals.append(total)
                for v in range(n_mem):
                    partial[it, l, v, jj] = jnp.concatenate(
                        [totals[0][v], totals[1][v]], 0
                    ).astype(jnp.bfloat16)

            for d in same_rows:
                part_copy(it, l, d).start()
            arrived[it, l, me_m] = partial[it, l, me_m]

        row_wait(*static_args(it))
        for l in range(2):
            diffuse_static(it, l)

        curv = jnp.zeros((8, LANES), jnp.float32)
        for l in range(2):
            bytes_wait(arrived.at[it, l], n_mem - 1, part_recv.at[it, l])
            total = arrived[it, l, 0].astype(jnp.float32)
            for v in range(1, n_mem):
                total = total + arrived[it, l, v].astype(jnp.float32)
            for j in range(tiles):
                part = total[j // 2, (j % 2) * 8:(j % 2) * 8 + 8]
                img = ens_coef * part + stat_part[l, j]
                image[l, j] = img
                cut = cutoff(l, j)
                misfit = 0.0 - lane_tile(observed, l, j)
                if it > 0:
                    misfit = increment[l, j] + misfit
                weight = cut / jnp.maximum(jnp.abs(misfit), jnp.where(cut == 0.0, 1.0, cut))
                curv = curv + weight * img * img

        first[it, my_plane] = jnp.concatenate(
            [
                jnp.sum(norm_acc[...], axis=0, keepdims=True),
                jnp.sum(curv, axis=0, keepdims=True),
            ],
            1,
        )
        for d in planes:
            first_copy(it, d).start()
        if it == 0:
            for j in range(tiles):
                image_all[me_m, j] = jnp.concatenate([image[0, j], image[1, j]], 0).astype(
                    jnp.bfloat16
                )
            for d in same_rows:
                gather_copy(image_all, image_send, image_recv, d).start()
        bytes_wait(first.at[it], n_first - 1, small_recv.at[it, 0])
        second[it, z] = jnp.sum(first[it], axis=0)
        for d in along_z:
            second_copy(it, d).start()
        if it == 0:
            for k in (1, 2):
                bytes_wait(seen_all, 3, obs_recv.at[k])
            bytes_wait(image_all, n_mem - 1, image_recv)
        else:
            for n, out in enumerate((control_o, grad_nat)):
                @pl.loop(0, 2)
                def _(l):
                    for r in range(rows):
                        for g in range(2):
                            value = [grad[n, l, SWEEPS + r, g, j] for j in range(tiles)]
                            for j, tile in enumerate(in_order(value)):
                                if n == 0:
                                    tile = 0.0 - step_ref[...] * tile
                                spread[l, j, r * 16 + g * 8:r * 16 + g * 8 + 8, :] = tile

                for j in range(tiles):
                    for l in range(2):
                        for k in range(16):
                            out[k, l, :, j * LANES:(j + 1) * LANES] = spread[
                                l, j, pl.ds(k, 8, stride=16), :
                            ]
        bytes_wait(second.at[it], n_second - 1, small_recv.at[it, 1])
        sums = jnp.sum(second[it], axis=0)
        norm = jnp.sum(sums[:, :LANES], axis=1, keepdims=True)
        curvature = jnp.sum(sums[:, LANES:], axis=1, keepdims=True)
        step = jnp.broadcast_to(norm / (norm + curvature), (8, LANES))
        if it == 0:
            step_ref[...] = step
            next_sent(1, step)
            static_source(1)
            increment[...] = 0.0 - step * image[...]
        else:
            @pl.loop(0, control_o.shape[0])
            def _(k):
                for l in range(2):
                    for j in range(tiles):
                        lanes = slice(j * LANES, (j + 1) * LANES)
                        control_o[k, l, :, lanes] = (
                            control_o[k, l, :, lanes] - step * grad_nat[k, l, :, lanes]
                        )
            for l in range(2):
                for j in range(tiles):
                    lanes = slice(j * LANES, (j + 1) * LANES)
                    own = slice(rows, 2 * rows)
                    static_o[l, :, lanes] = (
                        0.0 - step_ref[...] * stat_grad[0, l, j, own] - step * stat_grad[1, l, j, own]
                    )
                    increment_o[l, :, lanes] = increment[l, j] - step * image[l, j]

    row_wait_send(*index_args)
    bytes_wait(sent_all.at[0], n_mem - 1, sent_send)
    bytes_wait(image_all, n_mem - 1, image_send)
    seen_across().wait_send()
    for k in (1, 2):
        bytes_wait(seen_all, 3, obs_send.at[k])
    for it in range(ITERS):
        row_wait_send(*static_args(it))
        for l in range(2):
            for g in range(2):
                row_wait_send(*back_args(it, l, g))
            bytes_wait(arrived.at[it, l], n_mem - 1, part_send.at[it, l])
        bytes_wait(first.at[it], n_first - 1, small_send.at[it, 0])
        bytes_wait(second.at[it], n_second - 1, small_send.at[it, 1])


def local(n_mem, n_row, members, static_scale, observed, huber_class, scale_index):
    k, v, _, rows, cells = members.shape
    ens_coef = math.sqrt(0.7 / (k * n_mem - 1))
    f32, bf16 = jnp.float32, jnp.bfloat16
    tiles = cells // LANES
    V = pltpu.VMEM
    scratch = [
        V((tiles, k, v, 16, LANES), bf16),
        V((2, rows, cells), f32),
        V((2, rows, cells), f32),
        V((2, rows, cells), jnp.int32),
        V((2, rows, cells), jnp.int32),
        V((ITERS, n_mem, tiles, 16, LANES), bf16),
        V((ITERS, tiles, 16, LANES), bf16),
        V((ITERS, 2, tiles, 16, LANES), bf16),
        V((tiles, 16, LANES), bf16),
        V((2, tiles, 16, LANES), bf16),
        V((n_mem, 2 * tiles, 16, LANES), bf16),
        V((n_mem, tiles, 16, LANES), bf16),
        V((2, 3 * rows, tiles, 8, LANES), f32),
        V((2, tiles, 3 * rows, LANES), f32),
        V((2, tiles, k * rows, LANES), f32),
        V((2, 3 * rows, 2, tiles, 8, LANES), f32),
        V((ITERS, 2, 2, rows, tiles // 2, 16, LANES), bf16),
        V((ITERS, 2, 2, 2, rows, tiles // 2, 16, LANES), bf16),
        V((ITERS, 2, 2 * rows, 2, tiles, 8, LANES), f32),
        V((2, tiles, k * rows, LANES), f32),
        V((ITERS, 2, n_mem, tiles // 2, 16, LANES), bf16),
        V((ITERS, 2, n_mem, tiles // 2, 16, LANES), bf16),
        V((ITERS, 2, tiles, 3 * rows, LANES), f32),
        V((2, tiles, rows, LANES), f32),
        V((2, tiles, rows, LANES), f32),
        V((2, tiles, rows, LANES), f32),
        V((2, tiles, rows, LANES), f32),
        V((8, LANES), f32),
        V((8, LANES), f32),
        V((ITERS, 32, 1, 2 * LANES), f32),
        V((ITERS, 8, 1, 2 * LANES), f32),
        pltpu.SemaphoreType.DMA((4 + tiles,)),
        pltpu.SemaphoreType.DMA,
        pltpu.SemaphoreType.DMA,
        pltpu.SemaphoreType.DMA((ITERS * 5 + 1, 2)),
        pltpu.SemaphoreType.DMA((ITERS * 5 + 1, 2)),
        pltpu.SemaphoreType.DMA((ITERS, 2)),
        pltpu.SemaphoreType.DMA((ITERS, 2)),
        V((k, 2, rows, cells), f32),
        pltpu.SemaphoreType.DMA((ITERS, 2)),
        pltpu.SemaphoreType.DMA((ITERS, 2)),
        pltpu.SemaphoreType.DMA((3,)),
        pltpu.SemaphoreType.DMA((3,)),
        pltpu.SemaphoreType.DMA,
        pltpu.SemaphoreType.DMA,
    ]
    hbm = pl.BlockSpec(memory_space=pltpu.HBM)
    vmem = pl.BlockSpec(memory_space=pltpu.VMEM)
    wide = (k, 2, rows, cells)
    thin = (2, rows, cells)
    state = pl.pallas_call(
        functools.partial(kernel, n_mem, n_row, ens_coef),
        out_shape=[pltpu.VMEM(wide, f32), pltpu.VMEM(thin, f32), pltpu.VMEM(thin, f32)],
        in_specs=[hbm] * 5,
        out_specs=[vmem] * 3,
        scratch_shapes=scratch,
        compiler_params=pltpu.CompilerParams(
            collective_id=0, has_side_effects=True, vmem_limit_bytes=60 * 1024 * 1024
        ),
    )(
        members.reshape(k, v, 2 * rows, cells),
        static_scale[0],
        observed[0],
        huber_class[0],
        scale_index,
    )
    control, static_control, increment = state
    return control, static_control[None], increment[None]


def solution(mesh):
    sizes = dict(mesh.shape)
    placed = (
        P("mem", None, None, "row", None),
        P("mem", None, "row", None),
        P("mem", None, "row", None),
        P("mem", None, "row", None),
        P(None, "row", None),
    )
    return jax.shard_map(
        functools.partial(local, sizes["mem"], sizes["row"]),
        mesh=mesh,
        in_specs=placed,
        out_specs=(P("mem", None, "row", None),) * 3,
        check_vma=False,
    )
```

```python
import functools
import math

import jax
import jax.numpy as jnp
from jax import lax
from jax.experimental import pallas as pl
from jax.experimental.pallas import tpu as pltpu
from jax.sharding import PartitionSpec as P

SWEEPS = 4
ITERS = 2
KAPPAS = (0.06, 0.11, 0.17, 0.23)
LANES = 128
STAT = math.sqrt(0.3)
MESH = pl.DeviceIdType.MESH


def sideways(w):
    lane = lax.broadcasted_iota(jnp.int32, w.shape[1:], 1)[None]
    edge = jnp.zeros_like(w[:1])
    right = pltpu.roll(w, 1, 2)
    left = pltpu.roll(w, LANES - 1, 2)
    from_left = jnp.where(lane == 0, jnp.concatenate([edge, right[:-1]], 0), right)
    from_right = jnp.where(lane == LANES - 1, jnp.concatenate([left[1:], edge], 0), left)
    return from_left + from_right


def kernel(
    n_mem, n_row, ens_coef,
    members_h, scale_h, observed_h, huber_h, index_h,
    control_o, static_o, increment_o,
    members, scale, observed, huber, index,
    sent_all, send_static, static_halo, send_index, index_halo,
    seen_all, image_all,
    kwide, knat, turned, field, send_back, back_halo,
    grad, spread, partial, arrived,
    stat_grad, stat_back, stat_part, image, increment, norm_acc, step_ref, first, second,
    load_sem, sent_send, sent_recv, halo_send, halo_recv, part_send, part_recv,
    grad_nat, small_send, small_recv, obs_send, obs_recv, image_send, image_recv,
):
    me_m = lax.axis_index("mem")
    me_r = lax.axis_index("row")
    rows = 8
    tiles = 4
    has_low = me_r > 0
    has_high = me_r < n_row - 1

    def to(m, r):
        return {"mem": m, "row": r}

    loads = [
        pltpu.make_async_copy(observed_h, observed, load_sem.at[0]),
        pltpu.make_async_copy(huber_h, huber, load_sem.at[1]),
        pltpu.make_async_copy(index_h, index, load_sem.at[2]),
        pltpu.make_async_copy(scale_h, scale, load_sem.at[3]),
    ] + [
        pltpu.make_async_copy(
            members_h.at[:, :, :, pl.ds(j * LANES, LANES)], members.at[j], load_sem.at[4 + j]
        )
        for j in range(tiles)
    ]

    z_hi, y = me_m // 4, lax.rem(me_m, 4)
    x, z_lo, core = me_r // 8, lax.rem(me_r // 2, 4), lax.rem(me_r, 2)
    z = z_hi * 4 + z_lo

    def device_at(dx, dy, dz, dc):
        zz = lax.rem(z + dz, 8)
        m = (zz // 4) * 4 + lax.rem(y + dy, 4)
        r = lax.rem(x + dx, 4) * 8 + lax.rem(zz, 4) * 2 + lax.rem(core + dc, 2)
        return m, r

    def hops(d):
        return -(min(d[0], 4 - d[0]) + min(d[1], 4 - d[1]) + min(d[2], 8 - d[2]))

    planes = [(dx, dy, 0, dc) for dx in range(4) for dy in range(4) for dc in range(2)]
    planes = sorted(planes[1:], key=hops)
    along_z = sorted([(0, 0, dz, 0) for dz in range(1, 8)], key=hops)
    same_rows = sorted([(0, dy, dz, 0) for dz in (0, 4) for dy in range(4)][1:], key=hops)
    my_plane = (x * 4 + y) * 2 + core
    n_first, n_second = 32, 8

    greeted = sorted(set(planes + along_z + same_rows), key=hops)
    barrier = pltpu.get_barrier_semaphore()
    for d in greeted:
        pl.semaphore_signal(barrier, inc=1, device_id=to(*device_at(*d)), device_id_type=MESH)
    far = jnp.where(core == 0, me_r - 1, me_r + 1)
    has_far = jnp.logical_and(far >= 0, far < n_row)

    @pl.when(has_far)
    def _():
        pl.semaphore_signal(barrier, inc=1, device_id=to(me_m, far), device_id_type=MESH)

    for load in loads:
        load.start()

    def lane_tile(ref, l, j):
        return ref[l, :, j * LANES:(j + 1) * LANES]

    def cutoff(l, j):
        h = lane_tile(huber, l, j)
        return jnp.where(h == 1, 0.5, jnp.where(h == 2, 1.0, jnp.where(h == 3, 2.0, 0.0))).astype(
            jnp.float32
        )

    for load in loads[:4]:
        load.wait()
    for j in range(tiles):
        send_index[j] = jnp.concatenate(
            [lane_tile(index, 0, j), lane_tile(index, 1, j)], 0
        ).astype(jnp.float32).astype(jnp.bfloat16)

    @pl.when(jnp.logical_not(has_low))
    def _():
        index_halo[0] = jnp.full(index_halo.shape[1:], -1.0, jnp.bfloat16)
        static_halo[:, 0] = jnp.zeros_like(static_halo[:, 0])
        for it in range(ITERS):
            for l in range(2):
                for g in range(2):
                    back_halo[it, 0, l, g] = jnp.zeros_like(back_halo[it, 0, l, g])

    @pl.when(jnp.logical_not(has_high))
    def _():
        index_halo[1] = jnp.full(index_halo.shape[1:], -1.0, jnp.bfloat16)
        static_halo[:, 1] = jnp.zeros_like(static_halo[:, 1])
        for it in range(ITERS):
            for l in range(2):
                for g in range(2):
                    back_halo[it, 1, l, g] = jnp.zeros_like(back_halo[it, 1, l, g])

    def static_source(it):
        for j in range(tiles):
            wide = sent_all[it, me_m, j].astype(jnp.float32)
            for l in range(2):
                stat_back[l, j] = STAT * lane_tile(scale, l, j) * wide[l * rows:(l + 1) * rows]
            send_static[it, j] = jnp.concatenate(
                [stat_back[0, j], stat_back[1, j]], 0
            ).astype(jnp.bfloat16)

    def first_sent():
        for j in range(tiles):
            cut = jnp.concatenate([cutoff(0, j), cutoff(1, j)], 0)
            seen = jnp.concatenate([lane_tile(observed, 0, j), lane_tile(observed, 1, j)], 0)
            seen_all[me_m, j] = seen.astype(jnp.bfloat16)
            seen_all[me_m, tiles + j] = cut.astype(jnp.bfloat16)
            sent_all[0, me_m, j] = jnp.minimum(jnp.maximum(0.0 - seen, -cut), cut).astype(
                jnp.bfloat16
            )

    def next_sent(it, step):
        both = jnp.concatenate([step, step], 0)

        @pl.loop(0, n_mem)
        def _(v):
            for j in range(tiles):
                cut = seen_all[v, tiles + j].astype(jnp.float32)
                seen = seen_all[v, j].astype(jnp.float32)
                misfit = 0.0 - both * image_all[v, j].astype(jnp.float32) - seen
                sent_all[it, v, j] = jnp.minimum(jnp.maximum(misfit, -cut), cut).astype(
                    jnp.bfloat16
                )

    def rowcopy(src, dst_at, slot, side):
        target = me_r + 1 if side == 0 else me_r - 1
        return pltpu.make_async_remote_copy(
            src_ref=src, dst_ref=dst_at(side), send_sem=halo_send.at[slot, side],
            recv_sem=halo_recv.at[slot, side], device_id=to(me_m, target), device_id_type=MESH,
        )

    def row_start(src, dst_at, slot):
        @pl.when(has_high)
        def _():
            rowcopy(src, dst_at, slot, 0).start()

        @pl.when(has_low)
        def _():
            rowcopy(src, dst_at, slot, 1).start()

    def row_wait(src, dst_at, slot):
        @pl.when(has_low)
        def _():
            rowcopy(src, dst_at, slot, 0).wait_recv()

        @pl.when(has_high)
        def _():
            rowcopy(src, dst_at, slot, 1).wait_recv()

    def row_wait_send(src, dst_at, slot):
        @pl.when(has_high)
        def _():
            rowcopy(src, dst_at, slot, 0).wait_send()

        @pl.when(has_low)
        def _():
            rowcopy(src, dst_at, slot, 1).wait_send()

    n_slot = 5
    index_args = (send_index, lambda side: index_halo.at[side], ITERS * n_slot)

    def static_args(it):
        return send_static.at[it], lambda side: static_halo.at[it, side], it * n_slot

    def back_args(it, l, g):
        slot = it * n_slot + 1 + g * 2 + l
        return send_back.at[it, l, g], lambda side: back_halo.at[it, side, l, g], slot

    def push(src, dst, send, recv, device):
        return pltpu.make_async_remote_copy(
            src_ref=src, dst_ref=dst, send_sem=send, recv_sem=recv,
            device_id=to(*device), device_id_type=MESH,
        )

    def gather_copy(ref, send, recv, d):
        return push(ref.at[me_m], ref.at[me_m], send, recv, device_at(*d))

    def part_copy(it, l, d):
        v, r = device_at(*d)
        return push(
            partial.at[it, l, v], arrived.at[it, l, me_m],
            part_send.at[it, l], part_recv.at[it, l], (v, r),
        )

    def first_copy(it, d):
        own = first.at[it, my_plane]
        return push(own, own, small_send.at[it, 0], small_recv.at[it, 0], device_at(*d))

    def second_copy(it, d):
        own = second.at[it, z]
        return push(own, own, small_send.at[it, 1], small_recv.at[it, 1], device_at(*d))

    across = (0, 0, 4, 0)
    partner = lax.rem(me_m + 4, 8)
    along_y = [(0, dy, 0, 0) for dy in (2, 1, 3)]

    def seen_across():
        own = seen_all.at[me_m]
        return push(own, own, obs_send.at[0], obs_recv.at[0], device_at(*across))

    def seen_along(slot, k):
        own = seen_all.at[slot]
        return [push(own, own, obs_send.at[k], obs_recv.at[k], device_at(*d)) for d in along_y]

    def bytes_wait(ref, count, sem):
        part = ref.at[pl.ds(0, count)]
        pltpu.make_async_copy(part, part, sem).wait()

    def diffuse(it, l, g):
        low_in = jnp.where(has_low, 1.0, 0.0).astype(jnp.float32)
        high_in = jnp.where(has_high, 1.0, 0.0).astype(jnp.float32)
        for sweep in range(SWEEPS):
            lo, hi = sweep, 3 * rows - sweep

            def get(row):
                u = field[l, row, g]
                return u, u * kwide[l, row]

            _, w_prev = get(lo)
            u_cur, w_cur = get(lo + 1)
            norm = jnp.zeros((8, LANES), jnp.float32)
            for row in range(lo + 1, hi - 1):
                u_next, w_next = get(row + 1)
                out = (w_prev + w_next) + sideways(w_cur) + (u_cur - 4.0 * w_cur)
                if sweep < SWEEPS - 1:
                    field[l, row, g] = out
                else:
                    if it > 0:
                        out = out - step_ref[...] * grad[0, l, row - SWEEPS, g]
                    if row < rows:
                        out = out * low_in
                    elif row >= 2 * rows:
                        out = out * high_in
                    else:
                        norm = norm + jnp.sum(out * out, axis=0)
                    grad[it, l, row - SWEEPS, g] = out
                w_prev, u_cur, w_cur = w_cur, u_next, w_next
        norm_acc[...] += norm
        for sweep in range(SWEEPS):
            lo, hi = SWEEPS + sweep, 3 * rows - SWEEPS - sweep

            def load(row):
                return grad[it, l, row - SWEEPS, g] if sweep == 0 else field[l, row, g]

            u_prev, u_cur = load(lo), load(lo + 1)
            for row in range(lo + 1, hi - 1):
                u_next = load(row + 1)
                out = u_cur + kwide[l, row] * ((u_prev + u_next) + sideways(u_cur) - 4.0 * u_cur)
                if sweep < SWEEPS - 1:
                    field[l, row, g] = out
                else:
                    out = out.astype(jnp.bfloat16).astype(jnp.float32)
                    for j in range(tiles):
                        spread[l, j, pl.ds((row - rows) * 16 + g * 8, 8), :] = out[j]
                u_prev, u_cur = u_cur, u_next

    def diffuse_static(it, l):
        halo = static_halo[it].astype(jnp.float32)
        here = slice(l * rows, (l + 1) * rows)
        u = jnp.concatenate([halo[0, :, here], stat_back[l], halo[1, :, here]], 1)
        k = knat[l]
        grow = me_r * rows - rows + lax.broadcasted_iota(jnp.int32, (3 * rows, LANES), 0)
        inside = jnp.logical_and(grow >= 0, grow < n_row * rows)[None]
        n = 3 * rows
        for sweep in range(SWEEPS):
            w = k * u
            u = (pltpu.roll(w, 1, 1) + pltpu.roll(w, n - 1, 1)) + sideways(w) + (u - 4.0 * w)
        if it > 0:
            u = u - step_ref[:1] * stat_grad[0, l]
        u = jnp.where(inside, u, 0.0)
        stat_grad[it, l] = u
        own = u[:, rows:2 * rows]
        norm_acc[...] += jnp.sum(own * own, axis=0)
        for sweep in range(SWEEPS):
            u = u + k * (
                (pltpu.roll(u, 1, 1) + pltpu.roll(u, n - 1, 1)) + sideways(u) - 4.0 * u
            )
        for j in range(tiles):
            stat_part[l, j] = STAT * lane_tile(scale, l, j) * u[j, rows:2 * rows]

    first_sent()
    static_source(0)

    @pl.when(has_far)
    def _():
        pl.semaphore_wait(barrier, len(greeted) + 1)

    @pl.when(jnp.logical_not(has_far))
    def _():
        pl.semaphore_wait(barrier, len(greeted))

    for it in range(ITERS):
        if it == 0:
            for d in same_rows:
                gather_copy(sent_all.at[0], sent_send, sent_recv, d).start()
            row_start(*index_args)
            seen_across().start()
        row_start(*static_args(it))
        norm_acc[...] = jnp.zeros_like(norm_acc)
        if it == 0:
            row_wait(*index_args)
            for j in range(tiles):
                for l in range(2):
                    here = slice(l * rows, (l + 1) * rows)
                    both = index_halo[:, j].astype(jnp.float32)
                    ids = jnp.concatenate(
                        [both[0, here], lane_tile(index, l, j).astype(jnp.float32), both[1, here]],
                        0,
                    )
                    k = jnp.zeros_like(ids)
                    for i, value in enumerate(KAPPAS):
                        k = jnp.where(ids == i, value, k)
                    knat[l, j] = k
                    for row in range(3 * rows):
                        kwide[l, row, j] = jnp.broadcast_to(k[row:row + 1], (8, LANES))
            for load in loads[4:]:
                load.wait()
            bytes_wait(sent_all.at[0], n_mem - 1, sent_recv)

        for g in range(2):
            @pl.loop(0, tiles)
            def _(j):
                wide = [sent_all[it, v, j].astype(jnp.float32) for v in range(n_mem)]
                for k in range(g * 8, g * 8 + 8):
                    total = members[j, k, 0].astype(jnp.float32) * wide[0]
                    for v in range(1, n_mem):
                        total = total + members[j, k, v].astype(jnp.float32) * wide[v]
                    total = ens_coef * total
                    for l in range(2):
                        turned[l, j, k * 8:(k + 1) * 8, :] = total[l * rows:(l + 1) * rows]

            for l in range(2):
                @pl.loop(0, tiles // 2)
                def _(jj):
                    for r in range(rows):
                        pair_of = [
                            turned[l, jj * 2 + half, pl.ds(g * 64 + r, 8, stride=8), :]
                            for half in range(2)
                        ]
                        for half in range(2):
                            field[l, rows + r, g, jj * 2 + half] = pair_of[half]
                        send_back[it, l, g, r, jj] = jnp.concatenate(pair_of, 0).astype(
                            jnp.bfloat16
                        )

                row_start(*back_args(it, l, g))

        if it == 0:
            for copy in seen_along(me_m, 1):
                copy.start()
            seen_across().wait_recv()
            for copy in seen_along(partner, 2):
                copy.start()

        def arrive_and_diffuse(l, g):
            row_wait(*back_args(it, l, g))

            @pl.loop(0, rows)
            def _(r):
                for jj in range(tiles // 2):
                    for side in range(2):
                        value = back_halo[it, side, l, g, r, jj].astype(jnp.float32)
                        for half in range(2):
                            field[l, side * 2 * rows + r, g, jj * 2 + half] = value[
                                half * 8:(half + 1) * 8
                            ]

            diffuse(it, l, g)

        @pl.loop(0, 2)
        def _(l):
            arrive_and_diffuse(l, 0)

        for l in range(2):
            arrive_and_diffuse(l, 1)

            @pl.loop(0, tiles // 2)
            def _(jj):
                totals = []
                for half in range(2):
                    j = jj * 2 + half
                    total = [None] * n_mem
                    for k in range(16):
                        s = spread[l, j, pl.ds(k, 8, stride=16), :]
                        for v in range(n_mem):
                            m = members[j, k, v, l * rows:(l + 1) * rows, :].astype(jnp.float32)
                            total[v] = m * s if k == 0 else total[v] + m * s
                    totals.append(total)
                for v in range(n_mem):
                    partial[it, l, v, jj] = jnp.concatenate(
                        [totals[0][v], totals[1][v]], 0
                    ).astype(jnp.bfloat16)

            for d in same_rows:
                part_copy(it, l, d).start()
            arrived[it, l, me_m] = partial[it, l, me_m]

        row_wait(*static_args(it))
        for l in range(2):
            diffuse_static(it, l)

        curv = jnp.zeros((8, LANES), jnp.float32)
        for l in range(2):
            bytes_wait(arrived.at[it, l], n_mem - 1, part_recv.at[it, l])
            total = arrived[it, l, 0].astype(jnp.float32)
            for v in range(1, n_mem):
                total = total + arrived[it, l, v].astype(jnp.float32)
            for j in range(tiles):
                part = total[j // 2, (j % 2) * 8:(j % 2) * 8 + 8]
                img = ens_coef * part + stat_part[l, j]
                image[l, j] = img
                cut = cutoff(l, j)
                misfit = 0.0 - lane_tile(observed, l, j)
                if it > 0:
                    misfit = increment[l, j] + misfit
                weight = cut / jnp.maximum(jnp.abs(misfit), jnp.where(cut == 0.0, 1.0, cut))
                curv = curv + weight * img * img

        first[it, my_plane] = jnp.concatenate(
            [
                jnp.sum(norm_acc[...], axis=0, keepdims=True),
                jnp.sum(curv, axis=0, keepdims=True),
            ],
            1,
        )
        for d in planes:
            first_copy(it, d).start()
        if it == 0:
            for j in range(tiles):
                image_all[me_m, j] = jnp.concatenate([image[0, j], image[1, j]], 0).astype(
                    jnp.bfloat16
                )
            for d in same_rows:
                gather_copy(image_all, image_send, image_recv, d).start()
        bytes_wait(first.at[it], n_first - 1, small_recv.at[it, 0])
        second[it, z] = jnp.sum(first[it], axis=0)
        for d in along_z:
            second_copy(it, d).start()
        if it == 0:
            for k in (1, 2):
                bytes_wait(seen_all, 3, obs_recv.at[k])
            bytes_wait(image_all, n_mem - 1, image_recv)
        else:
            for n, out in enumerate((control_o, grad_nat)):
                @pl.loop(0, tiles)
                def _(j):
                    for l in range(2):
                        for r in range(rows):
                            for g in range(2):
                                value = grad[n, l, SWEEPS + r, g, j]
                                if n == 0:
                                    value = 0.0 - step_ref[...] * value
                                spread[l, j, r * 16 + g * 8:r * 16 + g * 8 + 8, :] = value

                for j in range(tiles):
                    for l in range(2):
                        for k in range(16):
                            out[k, l, :, j * LANES:(j + 1) * LANES] = spread[
                                l, j, pl.ds(k, 8, stride=16), :
                            ]
        bytes_wait(second.at[it], n_second - 1, small_recv.at[it, 1])
        sums = jnp.sum(second[it], axis=0)
        norm = jnp.sum(sums[:, :LANES], axis=1, keepdims=True)
        curvature = jnp.sum(sums[:, LANES:], axis=1, keepdims=True)
        step = jnp.broadcast_to(norm / (norm + curvature), (8, LANES))
        if it == 0:
            step_ref[...] = step
            next_sent(1, step)
            static_source(1)
            increment[...] = 0.0 - step * image[...]
        else:
            @pl.loop(0, control_o.shape[0])
            def _(k):
                for l in range(2):
                    for j in range(tiles):
                        lanes = slice(j * LANES, (j + 1) * LANES)
                        control_o[k, l, :, lanes] = (
                            control_o[k, l, :, lanes] - step * grad_nat[k, l, :, lanes]
                        )
            for l in range(2):
                for j in range(tiles):
                    lanes = slice(j * LANES, (j + 1) * LANES)
                    own = slice(rows, 2 * rows)
                    static_o[l, :, lanes] = (
                        0.0 - step_ref[...] * stat_grad[0, l, j, own] - step * stat_grad[1, l, j, own]
                    )
                    increment_o[l, :, lanes] = increment[l, j] - step * image[l, j]

    row_wait_send(*index_args)
    bytes_wait(sent_all.at[0], n_mem - 1, sent_send)
    bytes_wait(image_all, n_mem - 1, image_send)
    seen_across().wait_send()
    for k in (1, 2):
        bytes_wait(seen_all, 3, obs_send.at[k])
    for it in range(ITERS):
        row_wait_send(*static_args(it))
        for l in range(2):
            for g in range(2):
                row_wait_send(*back_args(it, l, g))
            bytes_wait(arrived.at[it, l], n_mem - 1, part_send.at[it, l])
        bytes_wait(first.at[it], n_first - 1, small_send.at[it, 0])
        bytes_wait(second.at[it], n_second - 1, small_send.at[it, 1])


def local(n_mem, n_row, members, static_scale, observed, huber_class, scale_index):
    k, v, _, rows, cells = members.shape
    ens_coef = math.sqrt(0.7 / (k * n_mem - 1))
    f32, bf16 = jnp.float32, jnp.bfloat16
    tiles = cells // LANES
    V = pltpu.VMEM
    scratch = [
        V((tiles, k, v, 16, LANES), bf16),
        V((2, rows, cells), f32),
        V((2, rows, cells), f32),
        V((2, rows, cells), jnp.int32),
        V((2, rows, cells), jnp.int32),
        V((ITERS, n_mem, tiles, 16, LANES), bf16),
        V((ITERS, tiles, 16, LANES), bf16),
        V((ITERS, 2, tiles, 16, LANES), bf16),
        V((tiles, 16, LANES), bf16),
        V((2, tiles, 16, LANES), bf16),
        V((n_mem, 2 * tiles, 16, LANES), bf16),
        V((n_mem, tiles, 16, LANES), bf16),
        V((2, 3 * rows, tiles, 8, LANES), f32),
        V((2, tiles, 3 * rows, LANES), f32),
        V((2, tiles, k * rows, LANES), f32),
        V((2, 3 * rows, 2, tiles, 8, LANES), f32),
        V((ITERS, 2, 2, rows, tiles // 2, 16, LANES), bf16),
        V((ITERS, 2, 2, 2, rows, tiles // 2, 16, LANES), bf16),
        V((ITERS, 2, 2 * rows, 2, tiles, 8, LANES), f32),
        V((2, tiles, k * rows, LANES), f32),
        V((ITERS, 2, n_mem, tiles // 2, 16, LANES), bf16),
        V((ITERS, 2, n_mem, tiles // 2, 16, LANES), bf16),
        V((ITERS, 2, tiles, 3 * rows, LANES), f32),
        V((2, tiles, rows, LANES), f32),
        V((2, tiles, rows, LANES), f32),
        V((2, tiles, rows, LANES), f32),
        V((2, tiles, rows, LANES), f32),
        V((8, LANES), f32),
        V((8, LANES), f32),
        V((ITERS, 32, 1, 2 * LANES), f32),
        V((ITERS, 8, 1, 2 * LANES), f32),
        pltpu.SemaphoreType.DMA((4 + tiles,)),
        pltpu.SemaphoreType.DMA,
        pltpu.SemaphoreType.DMA,
        pltpu.SemaphoreType.DMA((ITERS * 5 + 1, 2)),
        pltpu.SemaphoreType.DMA((ITERS * 5 + 1, 2)),
        pltpu.SemaphoreType.DMA((ITERS, 2)),
        pltpu.SemaphoreType.DMA((ITERS, 2)),
        V((k, 2, rows, cells), f32),
        pltpu.SemaphoreType.DMA((ITERS, 2)),
        pltpu.SemaphoreType.DMA((ITERS, 2)),
        pltpu.SemaphoreType.DMA((3,)),
        pltpu.SemaphoreType.DMA((3,)),
        pltpu.SemaphoreType.DMA,
        pltpu.SemaphoreType.DMA,
    ]
    hbm = pl.BlockSpec(memory_space=pltpu.HBM)
    vmem = pl.BlockSpec(memory_space=pltpu.VMEM)
    wide = (k, 2, rows, cells)
    thin = (2, rows, cells)
    state = pl.pallas_call(
        functools.partial(kernel, n_mem, n_row, ens_coef),
        out_shape=[pltpu.VMEM(wide, f32), pltpu.VMEM(thin, f32), pltpu.VMEM(thin, f32)],
        in_specs=[hbm] * 5,
        out_specs=[vmem] * 3,
        scratch_shapes=scratch,
        compiler_params=pltpu.CompilerParams(
            collective_id=0, has_side_effects=True, vmem_limit_bytes=60 * 1024 * 1024
        ),
    )(
        members.reshape(k, v, 2 * rows, cells),
        static_scale[0],
        observed[0],
        huber_class[0],
        scale_index,
    )
    control, static_control, increment = state
    return control, static_control[None], increment[None]


def solution(mesh):
    sizes = dict(mesh.shape)
    placed = (
        P("mem", None, None, "row", None),
        P("mem", None, "row", None),
        P("mem", None, "row", None),
        P("mem", None, "row", None),
        P(None, "row", None),
    )
    return jax.shard_map(
        functools.partial(local, sizes["mem"], sizes["row"]),
        mesh=mesh,
        in_specs=placed,
        out_specs=(P("mem", None, "row", None),) * 3,
        check_vma=False,
    )
```
